256 devices in a mesh: sx: 16 (over y, x), sy: 16 (over z, core).
Axes of the slice: x: 4, y: 4, z: 8, core: 2. Of those that a mesh axis runs over, the one named last changes fastest.
Arguments:
- points: bfloat16 [16, 16, 96, 1024], P('sx', 'sy'), may hold values from -6 to 6
- owners: int32 [16, 16, 1024, 1], P('sx', 'sy'), may hold values from 0 to 15; in each aligned block of 1024 rows (0 to 1023, 1024 to 2047, ..., all dimensions but the last counted through in order) at most 128 rows name the same one
- kernel_maps: int32 [16, 16, 27, 2048], P('sx', 'sy'), may hold values from 0 to 2560
- face_rows: int32 [16, 16, 2, 256], P('sx', 'sy'), may hold values from 0 to 2047
- weight: bfloat16 [27, 96, 96], replicated, may hold values from -0.15625 to 0.15625
- cotangent: bfloat16 [16, 16, 96, 2048], P('sx', 'sy'), may hold values from -6 to 6
Outputs:
- output: bfloat16 [16, 16, 96, 2048], P('sx', 'sy')
- point_grad: bfloat16 [16, 16, 96, 1024], P('sx', 'sy')
- weight_grad: float32 [27, 96, 96], replicated
The draws below stay inside these ranges and needn't reach their ends.
Inputs may be any that keep to these rules, and one draw needn't show every extreme that they name: `owners`: among the voxels of one device no owner is named more than 128 times, a bound that some block reaches.
All inputs are finite; a program needn't handle non-finite values.
Results may differ from the reference program's by a relative error of at most 0.005.
Values may be sent and summed in bfloat16 or wider, within the bound.
No kernel may reach another device: no remote copies, remote signals or barrier semaphores. Data moves between devices by JAX's collectives and lax.ppermute only.
A program may use at most 64 MiB of HBM per device.

```python
import math
import jax
import jax.numpy as jnp
import numpy as np
from jax import lax

C = 96
K = 27
R = 1024
F = 256
CAP = 128
V = 2048
N_SX = 16
N_SY = 16


def touch_ends(drawn, own_key, smallest, high):
    place = [jax.random.randint(jax.random.fold_in(own_key, axis), (), 0, length) for axis, length in enumerate(drawn.shape)]
    longest = drawn.shape.index(max(drawn.shape))
    next_to = place[:longest] + [(place[longest] + 1) % drawn.shape[longest]] + place[longest + 1:]
    return drawn.at[tuple(place)].set(smallest).at[tuple(next_to)].set(high)


def shard_levels(own_key, dims, cuts, smallest, high):
    gain = 1.0
    for dim, parts in cuts:
        heights = jax.random.uniform(jax.random.fold_in(jax.random.fold_in(own_key, 6), dim), (parts,), jnp.float32, smallest / len(cuts), high / len(cuts))
        gain = gain * jnp.repeat(jnp.exp(heights), dims[dim] // parts).reshape((-1,) + (1,) * (len(dims) - 1 - dim))
    return gain


def deal_out(rng, own, number, rows, count, top, limit, lean):
    order = jax.random.permutation(rng, count)
    crowded, ordinary = portions_of(count, rows * top, limit, lean, True), portions_of(count, rows * top, limit, lean, False)
    places = jnp.arange(count)

    def named(lengths, turn):
        used = int((lengths > 0).sum())
        fixed = max(1, used // 4)
        shifted = fixed + (places - fixed + turn * (used - fixed)) % max(1, count - fixed)
        return jnp.zeros((count,), jnp.int32).at[order[jnp.where(places < fixed, places, shifted)]].set(jnp.asarray(lengths, jnp.int32))

    lengths = jnp.where(number % 4 == 0, named(crowded, number // 4), named(ordinary, number - number // 4 - 1))
    mixed = jax.random.permutation(jax.random.fold_in(own, 3), count)
    source_of, taker = mixed[0:count // 2 * 2:2], mixed[1:count // 2 * 2:2]
    room = jnp.minimum(lengths[source_of] - 1, limit - lengths[taker]) // 2
    room = jnp.where((source_of == order[0]) | (taker == order[0]) | (lengths[taker] == 0), 0, jnp.maximum(room, 0))
    shifted = jax.random.randint(jax.random.fold_in(own, 4), (count // 2,), 0, 1 << 20) % (room + 1)
    lengths = lengths.at[source_of].add(-shifted).at[taker].add(shifted)
    labels = jnp.searchsorted(jnp.cumsum(lengths), jnp.arange(rows * top), side="right").astype(jnp.int32)
    table = labels.reshape(top, rows).T
    table = table[jax.random.permutation(jax.random.fold_in(own, 1), rows)]
    turn = jax.random.randint(jax.random.fold_in(own, 2), (rows, 1), 0, top)
    return jnp.take_along_axis(table, (jnp.arange(top)[None, :] + turn) % top, axis=1)


def portions_of(amount, total, most, lean, full):
    portions = [(1 << 20) // math.isqrt(grade ** lean) + 1 for grade in range(1, amount + 1)]
    largest = most if full else min(most, max(-(-total // amount), total * portions[0] // sum(portions)))
    least = 1 if total - largest >= amount - 1 else 0
    given, rest = [largest] + [least] * (amount - 1), total - largest - least * (amount - 1)
    while rest > 0:
        movable = [i for i in range(1, amount) if given[i] < largest] or [i for i in range(1, amount) if given[i] < most]
        pool, budget = sum([portions[i] for i in movable]), rest
        for i in movable:
            more = min(most - given[i], max(1, budget * portions[i] // pool), rest)
            given[i] = given[i] + more
            rest = rest - more
    return np.array(given)


def normal_values(rng, extent, scale, limit, shards=(), kind=jnp.bfloat16):
    drawn = jax.random.normal(rng, extent, jnp.float32) * scale
    if len(shards) > 0:
        drawn = shard_levels(rng, extent, shards, -0.22, 0.18) * drawn
    return jnp.clip(drawn, min=-limit, max=limit).astype(kind)


def setup_inputs(seed: int = 0) -> dict:
    key_of = jax.random.split(jax.random.key(seed), 7)
    points = normal_values(key_of[0], (N_SX, N_SY, C, R), 1.0, 6.0, ((0, 16), (1, 16)))
    owners_keys = jax.random.split(jax.random.fold_in(key_of[1], 1), N_SX * N_SY * R // R)
    owners_turns = jax.random.permutation(jax.random.fold_in(key_of[1], 3), N_SX * N_SY * R // R)
    owners = jax.vmap(lambda own, number: deal_out(jax.random.fold_in(key_of[1], 2), own, number, R, N_SX, 1, CAP, 2))(owners_keys, owners_turns).reshape((N_SX, N_SY, R, 1))
    kernel_maps = touch_ends(jax.random.randint(key_of[2], (N_SX, N_SY, K, V), 0, V + 2 * F + 1), jax.random.fold_in(key_of[2], 1), 0, V + 2 * F).astype(jnp.int32)
    face_rows = touch_ends(jax.random.randint(key_of[3], (N_SX, N_SY, 2, F), 0, V), jax.random.fold_in(key_of[3], 1), 0, V - 1).astype(jnp.int32)
    weight = normal_values(key_of[4], (K, C, C), (K * C // 2) ** -0.5, 0.15625)
    cotangent = normal_values(key_of[5], (N_SX, N_SY, C, V), 1.0, 6.0, ((0, 16), (1, 16)))
    return dict(points=points, owners=owners, kernel_maps=kernel_maps, face_rows=face_rows, weight=weight, cotangent=cotangent)


def silu_pair(preact):
    logistic = jax.nn.sigmoid(preact)
    return (preact * logistic, logistic * (1.0 + preact * (1.0 - logistic)))

def slot_positions(owner_of, groups, capacity):
    onehot = (owner_of[..., None] == jnp.arange(groups, dtype=jnp.int32)).astype(jnp.int32)
    before = jnp.cumsum(onehot, axis=-2) - onehot
    rank_in = lax.optimization_barrier(jnp.sum(before * onehot, axis=-1))
    return (owner_of * capacity + rank_in).astype(jnp.int32)

def device_pass(lookup, kernel_map, weight, incoming):
    channels = lookup.shape[0]
    owned_len = kernel_map.shape[1]

    def forward(running, pieces):
        columns, kernel = pieces
        picked = jnp.take(lookup, columns, axis=1)
        return (running + jnp.dot(kernel, picked, preferred_element_type=jnp.float32), None)
    preact = lax.scan(forward, jnp.zeros((channels, owned_len), jnp.float32), (kernel_map, weight))[0]
    activated, derivative = silu_pair(preact)
    output = activated.astype(jnp.bfloat16)
    grad_pre = (incoming.astype(jnp.float32) * derivative).astype(jnp.bfloat16)

    def backward(table_grad, pieces):
        columns, kernel = pieces
        picked = jnp.take(lookup, columns, axis=1)
        kernel_grad = lax.dot_general(grad_pre, picked, (((1,), (1,)), ((), ())), preferred_element_type=jnp.float32)
        spread = lax.dot_general(kernel, grad_pre, (((0,), (0,)), ((), ())), preferred_element_type=jnp.float32)
        return (table_grad.at[:, columns].add(spread), kernel_grad)
    table_grad, kernel_grads = lax.scan(backward, jnp.zeros((channels, lookup.shape[1]), jnp.float32), (kernel_map, weight))
    return (output, table_grad, kernel_grads)

def reference(points, owners, kernel_maps, face_rows, weight, cotangent):
    slot_pos = slot_positions(owners[..., 0], N_SX, CAP)

    def placed(columns, where):
        return jnp.zeros((C, V), jnp.bfloat16).at[:, where].set(columns)
    outgoing = jax.vmap(jax.vmap(placed))(points, slot_pos)
    owned = jnp.transpose(outgoing.reshape(N_SX, N_SY, C, N_SX, CAP), (3, 1, 2, 0, 4)).reshape(N_SX, N_SY, C, V)

    def take_faces(own_block, face_list):
        return jnp.take(own_block, face_list, axis=1)
    faces = jax.vmap(jax.vmap(take_faces))(owned, face_rows)
    zero_face = jnp.zeros((N_SX, 1, C, F), jnp.bfloat16)
    ghost_low = jnp.concatenate([zero_face, faces[:, :-1, :, 1]], axis=1)
    ghost_high = jnp.concatenate([faces[:, 1:, :, 0], zero_face], axis=1)
    lookup = jnp.concatenate([owned, ghost_low, ghost_high, jnp.zeros((N_SX, N_SY, C, 1), jnp.bfloat16)], axis=-1)
    wide = V + 2 * F + 1

    def per_device(weight_sum, pieces):
        output, table_grad, kernel_grads = device_pass(pieces[0], pieces[1], weight, pieces[2])
        return (weight_sum + kernel_grads, (output, table_grad))
    weight_sum, (outputs, table_grads) = lax.scan(per_device, jnp.zeros((K, C, C), jnp.float32), (lookup.reshape(N_SX * N_SY, C, wide), kernel_maps.reshape(N_SX * N_SY, K, V), cotangent.reshape(N_SX * N_SY, C, V)))
    table_grads = table_grads.reshape(N_SX, N_SY, C, wide)
    grad_low = table_grads[..., V:V + F]
    grad_high = table_grads[..., V + F:V + 2 * F]
    zero_grad = jnp.zeros((N_SX, 1, C, F), jnp.float32)
    recv_low = jnp.concatenate([zero_grad, grad_high[:, :-1]], axis=1)
    recv_high = jnp.concatenate([grad_low[:, 1:], zero_grad], axis=1)

    def fold_faces(own_grad, face_list, lower, upper):
        return own_grad.at[:, face_list[0]].add(lower).at[:, face_list[1]].add(upper)
    owned_grad = jax.vmap(jax.vmap(fold_faces))(table_grads[..., :V], face_rows, recv_low, recv_high).astype(jnp.bfloat16)
    returned = jnp.transpose(owned_grad.reshape(N_SX, N_SY, C, N_SX, CAP), (3, 1, 2, 0, 4)).reshape(N_SX, N_SY, C, V)

    def take_back(block, where):
        return jnp.take(block, where, axis=1)
    point_grad = jax.vmap(jax.vmap(take_back))(returned, slot_pos)
    weight_grad = weight_sum * (1.0 / math.sqrt(N_SX * N_SY * V))
    return (outputs.reshape(N_SX, N_SY, C, V), point_grad, weight_grad)
```

```python
import math

import jax
import jax.numpy as jnp
from jax import lax
from jax.experimental import pallas as pl
from jax.experimental.pallas import tpu as pltpu
from jax.sharding import PartitionSpec as P

C = 96
K = 27
R = 1024
F = 256
CAP = 128
V = 2048
GROUPS = 16
LO = 256
BANKS = V // LO
ALL_BANKS = BANKS + 2
VB = 256
PER_DOT = 3

BF = jnp.bfloat16
F32 = jnp.float32
NT = (((1,), (1,)), ((), ()))


def onehot_rows(low, rows):
    row = lax.broadcasted_iota(jnp.int32, (rows, low.shape[-1]), 0)
    return jnp.where(row == low, 1.0, 0.0).astype(BF)


def select_banks(product, bank, banks):
    n = bank.shape[-1]
    bank8 = jnp.broadcast_to(bank, (8, n))
    kept = jnp.zeros((C // 8, 8, n), F32)
    for a in range(banks):
        part = product[a * C : (a + 1) * C].reshape(C // 8, 8, n)
        kept = jnp.where((bank8 == a)[None], part, kept)
    return kept.reshape(C, n)


def masked_banks(values, bank, banks, out_ref, column):
    n = bank.shape[-1]
    for a in range(banks):
        mask = jnp.where(jnp.broadcast_to(bank, (16, n)) == a, 1.0, 0.0).astype(BF)
        spread = values.reshape(C // 16, 16, n) * mask[None]
        out_ref[a * C : (a + 1) * C, column : column + n] = spread.reshape(C, n)


def place_kernel(points_ref, owner_ref, out_ref, slot_ref, masked_ref):
    owner = owner_ref[...]
    row = lax.broadcasted_iota(jnp.int32, (CAP, CAP), 0)
    col = lax.broadcasted_iota(jnp.int32, (CAP, CAP), 1)
    earlier = jnp.where(row < col, 1.0, 0.0).astype(BF)
    group = lax.broadcasted_iota(jnp.int32, (GROUPS, CAP), 0)
    total = jnp.zeros((GROUPS, 1), F32)
    for b in range(R // CAP):
        mine = jnp.where(group == owner[:, b * CAP : (b + 1) * CAP], 1.0, 0.0)
        before = jnp.dot(mine.astype(BF), earlier, preferred_element_type=F32) + total
        slot = jnp.sum(mine * before, axis=0, keepdims=True)
        slot_ref[:, b * CAP : (b + 1) * CAP] = slot.astype(jnp.int32)
        total = total + jnp.sum(mine, axis=1, keepdims=True)
    masked_banks(points_ref[...], owner, GROUPS, masked_ref, 0)
    onehot = onehot_rows(slot_ref[...], CAP)
    for g in range(GROUPS):
        out_ref[g] = lax.dot_general(
            masked_ref[g * C : (g + 1) * C, :], onehot, NT, preferred_element_type=F32
        ).astype(BF)


def place_points(points, owner):
    return pl.pallas_call(
        place_kernel,
        out_shape=(
            jax.ShapeDtypeStruct((GROUPS, C, CAP), BF),
            jax.ShapeDtypeStruct((1, R), jnp.int32),
        ),
        scratch_shapes=[pltpu.VMEM((GROUPS * C, R), BF)],
        compiler_params=pltpu.CompilerParams(vmem_limit_bytes=48 << 20),
        name="place",
    )(points, owner)


def faces_kernel(owned_ref, rows_ref, lower_ref, upper_ref):
    table = owned_ref[...].reshape(GROUPS * C, CAP)
    for j, out_ref in enumerate((lower_ref, upper_ref)):
        rows = rows_ref[j : j + 1, :]
        product = jnp.dot(table, onehot_rows(rows & (CAP - 1), CAP), preferred_element_type=F32)
        out_ref[...] = select_banks(product, rows >> 7, GROUPS).astype(BF)


def take_faces(owned, face_rows):
    return pl.pallas_call(
        faces_kernel,
        out_shape=(jax.ShapeDtypeStruct((C, F), BF),) * 2,
        compiler_params=pltpu.CompilerParams(vmem_limit_bytes=48 << 20),
        name="faces",
    )(owned, face_rows)


def forward_kernel(
    owned_ref, low_ref, high_ref, map_ref, weight_ref, cot_ref, out_ref, pre_ref, wg_ref, table_ref, picked_ref, acc_ref
):
    step = pl.program_id(0)

    @pl.when(step == 0)
    def _():
        for g in range(GROUPS):
            table_ref[(g // 2) * C : (g // 2 + 1) * C, (g % 2) * CAP : (g % 2 + 1) * CAP] = owned_ref[g]
        table_ref[BANKS * C : (BANKS + 1) * C, :] = low_ref[...]
        table_ref[(BANKS + 1) * C :, :] = high_ref[...]
        acc_ref[...] = jnp.zeros_like(acc_ref)

    table = table_ref[...]
    for k in range(K):
        index = map_ref[k]
        product = jnp.dot(table, onehot_rows(index & (LO - 1), LO), preferred_element_type=F32)
        picked_ref[k * C : (k + 1) * C, :] = select_banks(product, index >> 8, ALL_BANKS).astype(BF)
    preact = jnp.dot(weight_ref[...], picked_ref[...], preferred_element_type=F32)
    logistic = jax.nn.sigmoid(preact)
    out_ref[...] = (preact * logistic).astype(BF)
    slope = logistic * (1.0 + preact * (1.0 - logistic))
    grad_pre = (cot_ref[...].astype(F32) * slope).astype(BF)
    pre_ref[...] = grad_pre
    acc_ref[...] += lax.dot_general(picked_ref[...], grad_pre, NT, preferred_element_type=F32)

    @pl.when(step == pl.num_programs(0) - 1)
    def _():
        for k in range(K):
            wg_ref[k] = acc_ref[k * C : (k + 1) * C, :].T


def forward_pass(owned, low, high, kernel_map, weight, cotangent):
    whole = lambda *shape: pl.BlockSpec(shape, lambda i: (0,) * len(shape))
    column = lambda rows: pl.BlockSpec((rows, VB), lambda i: (0, i))
    return pl.pallas_call(
        forward_kernel,
        grid=(V // VB,),
        in_specs=[
            whole(GROUPS, C, CAP),
            whole(C, F),
            whole(C, F),
            pl.BlockSpec((K, 1, VB), lambda i: (0, 0, i)),
            whole(C, K * C),
            column(C),
        ],
        out_specs=(column(C), column(C), whole(K, C, C)),
        out_shape=(
            jax.ShapeDtypeStruct((C, V), BF),
            jax.ShapeDtypeStruct((C, V), BF),
            jax.ShapeDtypeStruct((K, C, C), F32),
        ),
        scratch_shapes=[
            pltpu.VMEM((ALL_BANKS * C, LO), BF),
            pltpu.VMEM((K * C, VB), BF),
            pltpu.VMEM((K * C, C), F32),
        ],
        compiler_params=pltpu.CompilerParams(vmem_limit_bytes=56 << 20),
        cost_estimate=pl.CostEstimate(
            flops=2 * K * V * ALL_BANKS * C * LO, bytes_accessed=4 << 20, transcendentals=C * V
        ),
        name="gather_forward",
    )(owned, low, high, kernel_map, weight, cotangent)


def scatter_kernel(map_ref, weight_ref, pre_ref, own_ref, low_ref, high_ref, spread_ref, masked_ref, acc_ref):
    step = pl.program_id(0)

    @pl.when(step == 0)
    def _():
        acc_ref[...] = jnp.zeros_like(acc_ref)

    spread_ref[...] = jnp.dot(weight_ref[...], pre_ref[...], preferred_element_type=F32).astype(BF)
    for first in range(0, K, PER_DOT):
        hots = []
        for j in range(PER_DOT):
            k = first + j
            index = map_ref[k]
            masked_banks(spread_ref[k * C : (k + 1) * C, :], index >> 8, ALL_BANKS, masked_ref, j * VB)
            hots.append(onehot_rows(index & (LO - 1), LO))
        acc_ref[...] += lax.dot_general(
            masked_ref[...], jnp.concatenate(hots, axis=1), NT, preferred_element_type=F32
        )

    @pl.when(step == pl.num_programs(0) - 1)
    def _():
        own_ref[...] = acc_ref[: BANKS * C, :]
        low_ref[...] = acc_ref[BANKS * C : (BANKS + 1) * C, :].astype(BF)
        high_ref[...] = acc_ref[(BANKS + 1) * C :, :].astype(BF)


def scatter_pass(kernel_map, weight, grad_pre):
    whole = lambda *shape: pl.BlockSpec(shape, lambda i: (0,) * len(shape))
    column = lambda rows: pl.BlockSpec((rows, VB), lambda i: (0, i))
    return pl.pallas_call(
        scatter_kernel,
        grid=(V // VB,),
        in_specs=[pl.BlockSpec((K, 1, VB), lambda i: (0, 0, i)), whole(K * C, C), column(C)],
        out_specs=(whole(BANKS * C, LO), whole(C, F), whole(C, F)),
        out_shape=(
            jax.ShapeDtypeStruct((BANKS * C, LO), F32),
            jax.ShapeDtypeStruct((C, F), BF),
            jax.ShapeDtypeStruct((C, F), BF),
        ),
        scratch_shapes=[
            pltpu.VMEM((K * C, VB), BF),
            pltpu.VMEM((ALL_BANKS * C, PER_DOT * VB), BF),
            pltpu.VMEM((ALL_BANKS * C, LO), F32),
        ],
        compiler_params=pltpu.CompilerParams(vmem_limit_bytes=56 << 20),
        cost_estimate=pl.CostEstimate(
            flops=2 * K * V * ALL_BANKS * C * LO, bytes_accessed=2 << 20, transcendentals=0
        ),
        name="scatter_backward",
    )(kernel_map, weight, grad_pre)


def fold_kernel(grad_ref, from_low_ref, from_high_ref, rows_ref, out_ref, masked_ref):
    hots = []
    for j, part_ref in enumerate((from_low_ref, from_high_ref)):
        rows = rows_ref[j : j + 1, :]
        masked_banks(part_ref[...], rows >> 8, BANKS, masked_ref, j * F)
        hots.append(onehot_rows(rows & (LO - 1), LO))
    folded = lax.dot_general(
        masked_ref[...], jnp.concatenate(hots, axis=1), NT, preferred_element_type=F32
    )
    total = (grad_ref[...] + folded).astype(BF)
    for g in range(GROUPS):
        out_ref[g] = total[(g // 2) * C : (g // 2 + 1) * C, (g % 2) * CAP : (g % 2 + 1) * CAP]


def fold_faces(table_grad, from_low, from_high, face_rows):
    return pl.pallas_call(
        fold_kernel,
        out_shape=jax.ShapeDtypeStruct((GROUPS, C, CAP), BF),
        scratch_shapes=[pltpu.VMEM((BANKS * C, 2 * F), BF)],
        compiler_params=pltpu.CompilerParams(vmem_limit_bytes=48 << 20),
        name="fold",
    )(table_grad, from_low, from_high, face_rows)


def take_back_kernel(back_ref, owner_ref, slot_ref, out_ref):
    table = back_ref[...].reshape(GROUPS * C, CAP)
    for b in range(R // LO):
        cols = slice(b * LO, (b + 1) * LO)
        product = jnp.dot(table, onehot_rows(slot_ref[:, cols], CAP), preferred_element_type=F32)
        out_ref[:, cols] = select_banks(product, owner_ref[:, cols], GROUPS).astype(BF)


def take_back(returned, owner, slot):
    return pl.pallas_call(
        take_back_kernel,
        out_shape=jax.ShapeDtypeStruct((C, R), BF),
        compiler_params=pltpu.CompilerParams(vmem_limit_bytes=48 << 20),
        name="take_back",
    )(returned, owner, slot)


def body(points, owners, kernel_maps, face_rows, weight, cotangent):
    points, owner = points[0, 0], owners.reshape(1, R)
    kernel_map, face_list, incoming = kernel_maps.reshape(K, 1, V), face_rows[0, 0], cotangent[0, 0]
    side = lax.axis_size("sy")
    up = [(i, i + 1) for i in range(side - 1)]
    down = [(i + 1, i) for i in range(side - 1)]

    outgoing, slot = place_points(points, owner)
    owned = lax.all_to_all(outgoing, "sx", 0, 0, tiled=True)
    lower, upper = take_faces(owned, face_list)
    ghost_low = lax.ppermute(upper, "sy", up)
    ghost_high = lax.ppermute(lower, "sy", down)
    weight_rows = jnp.transpose(weight, (1, 0, 2)).reshape(C, K * C)
    output, grad_pre, weight_part = forward_pass(
        owned, ghost_low, ghost_high, kernel_map, weight_rows, incoming
    )
    weight_grad = lax.psum(weight_part, ("sx", "sy")) * (1.0 / math.sqrt(GROUPS * side * V))
    weight_columns = jnp.transpose(weight, (0, 2, 1)).reshape(K * C, C)
    table_grad, to_low, to_high = scatter_pass(kernel_map, weight_columns, grad_pre)
    from_low = lax.ppermute(to_high, "sy", up)
    from_high = lax.ppermute(to_low, "sy", down)
    owned_grad = fold_faces(table_grad, from_low, from_high, face_list)
    returned = lax.all_to_all(owned_grad, "sx", 0, 0, tiled=True)
    point_grad = take_back(returned, owner, slot)
    return (output[None, None], point_grad[None, None], weight_grad)


def solution(mesh):
    split = P("sx", "sy", None, None)
    return jax.shard_map(
        body,
        mesh=mesh,
        in_specs=(split, split, split, split, P(), split),
        out_specs=(split, split, P()),
        check_vma=False,
    )
```

```python
import functools
import math

import jax
import jax.numpy as jnp
from jax import lax
from jax.experimental import pallas as pl
from jax.experimental.pallas import tpu as pltpu
from jax.sharding import PartitionSpec as P

C = 96
K = 27
R = 1024
F = 256
CAP = 128
V = 2048
GROUPS = 16
LO = 256
BANKS = V // LO
ALL_BANKS = BANKS + 2
WIDE = 512
WIDE_BANKS = ALL_BANKS * LO // WIDE
VB = 256
PER_DOT = 9
PARTS = (4, 3, 1)
LANES = 128
TILES = K * C // LANES
SLOTS = C // 8 * TILES // GROUPS

BF = jnp.bfloat16
F32 = jnp.float32
NT = (((1,), (1,)), ((), ()))


def rows16(index):
    return jnp.broadcast_to(index, (16, index.shape[-1])).astype(jnp.int16)


def onehot_rows(low, rows):
    n = low.shape[-1]
    row = lax.broadcasted_iota(jnp.int16, (rows, n), 0).reshape(rows // 16, 16, n)
    return jnp.where(row == rows16(low)[None], BF(1), BF(0)).reshape(rows, n)


def select_banks(product, bank, banks):
    n = bank.shape[-1]
    bank8 = jnp.broadcast_to(bank, (8, n))
    kept = jnp.zeros((C // 8, 8, n), F32)
    for a in range(banks):
        part = product[a * C : (a + 1) * C].reshape(C // 8, 8, n)
        kept = jnp.where((bank8 == a)[None], part, kept)
    return kept.reshape(C, n)


def masked_banks(values, bank, banks, out_ref, column):
    n = bank.shape[-1]
    bank16 = rows16(bank)
    values = values.reshape(C // 16, 16, n)
    for a in range(banks):
        spread = jnp.where((bank16 == a)[None], values, BF(0))
        out_ref[a * C : (a + 1) * C, column : column + n] = spread.reshape(C, n)


def place_kernel(points_ref, owner_ref, out_ref, slot_ref, masked_ref):
    owner = owner_ref[...]
    row = lax.broadcasted_iota(jnp.int32, (CAP, CAP), 0)
    col = lax.broadcasted_iota(jnp.int32, (CAP, CAP), 1)
    earlier = jnp.where(row < col, 1.0, 0.0).astype(BF)
    group = lax.broadcasted_iota(jnp.int32, (GROUPS, CAP), 0)
    total = jnp.zeros((GROUPS, 1), F32)
    for b in range(R // CAP):
        mine = jnp.where(group == owner[:, b * CAP : (b + 1) * CAP], 1.0, 0.0)
        before = jnp.dot(mine.astype(BF), earlier, preferred_element_type=F32) + total
        slot = jnp.sum(mine * before, axis=0, keepdims=True)
        slot_ref[:, b * CAP : (b + 1) * CAP] = slot.astype(jnp.int32)
        total = total + jnp.sum(mine, axis=1, keepdims=True)
    masked_banks(points_ref[...], owner, GROUPS, masked_ref, 0)
    onehot = onehot_rows(slot_ref[...], CAP)
    for g in range(GROUPS):
        out_ref[g] = lax.dot_general(
            masked_ref[g * C : (g + 1) * C, :], onehot, NT, preferred_element_type=F32
        ).astype(BF)


def place_points(points, owner):
    return pl.pallas_call(
        place_kernel,
        out_shape=(
            jax.ShapeDtypeStruct((GROUPS, C, CAP), BF),
            jax.ShapeDtypeStruct((1, R), jnp.int32),
        ),
        scratch_shapes=[pltpu.VMEM((GROUPS * C, R), BF)],
        compiler_params=pltpu.CompilerParams(vmem_limit_bytes=48 << 20),
        name="place",
    )(points, owner)


def faces_kernel(owned_ref, rows_ref, lower_ref, upper_ref):
    table = owned_ref[...].reshape(GROUPS * C, CAP)
    for j, out_ref in enumerate((lower_ref, upper_ref)):
        rows = rows_ref[j : j + 1, :]
        product = jnp.dot(table, onehot_rows(rows & (CAP - 1), CAP), preferred_element_type=F32)
        out_ref[...] = select_banks(product, rows >> 7, GROUPS).astype(BF)


def take_faces(owned, face_rows):
    return pl.pallas_call(
        faces_kernel,
        out_shape=(jax.ShapeDtypeStruct((C, F), BF),) * 2,
        compiler_params=pltpu.CompilerParams(vmem_limit_bytes=48 << 20),
        name="faces",
    )(owned, face_rows)


def forward_kernel(
    owned_ref, low_ref, high_ref, map_ref, weight_ref, cot_ref, out_ref, pre_ref, wg_ref, table_ref, picked_ref, acc_ref
):
    step = pl.program_id(0)

    @pl.when(step == 0)
    def _():
        per = WIDE // CAP
        for g in range(GROUPS):
            table_ref[(g // per) * C : (g // per + 1) * C, (g % per) * CAP : (g % per + 1) * CAP] = owned_ref[g]
        table_ref[(WIDE_BANKS - 1) * C :, :F] = low_ref[...]
        table_ref[(WIDE_BANKS - 1) * C :, F:] = high_ref[...]
        acc_ref[...] = jnp.zeros_like(acc_ref)

    table = table_ref[...]
    for k in range(K):
        index = map_ref[k]
        product = jnp.dot(table, onehot_rows(index & (WIDE - 1), WIDE), preferred_element_type=F32)
        picked_ref[k * C : (k + 1) * C, :] = select_banks(product, index >> 9, WIDE_BANKS).astype(BF)
    preact = jnp.dot(weight_ref[...], picked_ref[...], preferred_element_type=F32)
    logistic = jax.nn.sigmoid(preact)
    out_ref[...] = (preact * logistic).astype(BF)
    slope = logistic * (1.0 + preact * (1.0 - logistic))
    grad_pre = (cot_ref[...].astype(F32) * slope).astype(BF)
    pre_ref[...] = grad_pre
    acc_ref[...] += lax.dot_general(picked_ref[...], grad_pre, NT, preferred_element_type=F32)

    @pl.when(step == pl.num_programs(0) - 1)
    def _():
        for t in range(TILES):
            block = acc_ref[t * LANES : (t + 1) * LANES, :].T
            for i in range(C // 8):
                shard, slot = divmod(i * TILES + t, SLOTS)
                wg_ref[shard, slot * 8 : (slot + 1) * 8, :] = block[i * 8 : (i + 1) * 8, :]
        rest = acc_ref[TILES * LANES :, :].T
        rest = jnp.concatenate([rest, jnp.zeros((C, LANES - rest.shape[1]), F32)], axis=1)
        for g in range(GROUPS):
            tail = rest[g * 8 : (g + 1) * 8, :] if g < C // 8 else jnp.zeros((8, LANES), F32)
            wg_ref[g, SLOTS * 8 :, :] = tail


def forward_pass(owned, low, high, kernel_map, weight, cotangent):
    whole = lambda *shape: pl.BlockSpec(shape, lambda i: (0,) * len(shape))
    column = lambda rows: pl.BlockSpec((rows, VB), lambda i: (0, i))
    return pl.pallas_call(
        forward_kernel,
        grid=(V // VB,),
        in_specs=[
            whole(GROUPS, C, CAP),
            whole(C, F),
            whole(C, F),
            pl.BlockSpec((K, 1, VB), lambda i: (0, 0, i)),
            whole(C, K * C),
            column(C),
        ],
        out_specs=(column(C), column(C), whole(GROUPS, LANES, LANES)),
        out_shape=(
            jax.ShapeDtypeStruct((C, V), BF),
            jax.ShapeDtypeStruct((C, V), BF),
            jax.ShapeDtypeStruct((GROUPS, LANES, LANES), F32),
        ),
        scratch_shapes=[
            pltpu.VMEM((WIDE_BANKS * C, WIDE), BF),
            pltpu.VMEM((K * C, VB), BF),
            pltpu.VMEM((K * C, C), F32),
        ],
        compiler_params=pltpu.CompilerParams(vmem_limit_bytes=56 << 20),
        cost_estimate=pl.CostEstimate(
            flops=2 * K * V * ALL_BANKS * C * LO, bytes_accessed=4 << 20, transcendentals=C * V
        ),
        name="gather_forward",
    )(owned, low, high, kernel_map, weight, cotangent)


def scatter_step(map_ref, weight_ref, pre_ref, acc_ref, spread_ref, masked_ref):
    spread_ref[...] = jnp.dot(weight_ref[...], pre_ref[...], preferred_element_type=F32).astype(BF)
    for first in range(0, K, PER_DOT):
        hots = []
        for j in range(PER_DOT):
            k = first + j
            index = map_ref[k]
            masked_banks(spread_ref[k * C : (k + 1) * C, :], index >> 8, ALL_BANKS, masked_ref, j * VB)
            hots.append(onehot_rows(index & (LO - 1), LO))
        acc_ref[...] += lax.dot_general(
            masked_ref[...], jnp.concatenate(hots, axis=1), NT, preferred_element_type=F32
        )


def scatter_kernel(
    has_start, has_faces, after_ref, start_ref, map_ref, weight_ref, pre_ref, *refs
):
    if has_faces:
        own_ref, low_ref, high_ref, spread_ref, masked_ref, acc_ref = refs
    else:
        acc_ref, spread_ref, masked_ref = refs

    @pl.when(pl.program_id(0) == 0)
    def _():
        acc_ref[...] = start_ref[...] if has_start else jnp.zeros_like(acc_ref)

    scatter_step(map_ref, weight_ref, pre_ref, acc_ref, spread_ref, masked_ref)

    if has_faces:

        @pl.when(pl.program_id(0) == pl.num_programs(0) - 1)
        def _():
            own_ref[...] = acc_ref[: BANKS * C, :]
            low_ref[...] = acc_ref[BANKS * C : (BANKS + 1) * C, :].astype(BF)
            high_ref[...] = acc_ref[(BANKS + 1) * C :, :].astype(BF)


def scatter_part(part, after, start, kernel_map, weight, grad_pre):
    whole = lambda *shape: pl.BlockSpec(shape, lambda i: (0,) * len(shape))
    sums = jax.ShapeDtypeStruct((ALL_BANKS * C, LO), F32)
    scratch = [pltpu.VMEM((K * C, VB), BF), pltpu.VMEM((ALL_BANKS * C, PER_DOT * VB), BF)]
    at, steps, last = sum(PARTS[:part]), PARTS[part], part == len(PARTS) - 1
    if last:
        out_specs = (whole(BANKS * C, LO), whole(C, F), whole(C, F))
        out_shape = (
            jax.ShapeDtypeStruct((BANKS * C, LO), F32),
            jax.ShapeDtypeStruct((C, F), BF),
            jax.ShapeDtypeStruct((C, F), BF),
        )
        scratch.append(pltpu.VMEM(sums.shape, F32))
    else:
        out_specs, out_shape = whole(*sums.shape), sums
    return pl.pallas_call(
        functools.partial(scatter_kernel, part > 0, last),
        grid=(steps,),
        in_specs=[
            pl.BlockSpec(memory_space=pl.ANY),
            whole(*sums.shape) if part > 0 else pl.BlockSpec(memory_space=pl.ANY),
            pl.BlockSpec((K, 1, VB), lambda i: (0, 0, at + i)),
            whole(K * C, C),
            pl.BlockSpec((C, VB), lambda i: (0, at + i)),
        ],
        out_specs=out_specs,
        out_shape=out_shape,
        scratch_shapes=scratch,
        compiler_params=pltpu.CompilerParams(vmem_limit_bytes=56 << 20),
        cost_estimate=pl.CostEstimate(
            flops=2 * K * VB * steps * ALL_BANKS * C * LO, bytes_accessed=2 << 20, transcendentals=0
        ),
        name="scatter",
    )(after, start, kernel_map, weight, grad_pre)


def fold_kernel(grad_ref, from_low_ref, from_high_ref, rows_ref, out_ref, masked_ref):
    hots = []
    for j, part_ref in enumerate((from_low_ref, from_high_ref)):
        rows = rows_ref[j : j + 1, :]
        masked_banks(part_ref[...], rows >> 8, BANKS, masked_ref, j * F)
        hots.append(onehot_rows(rows & (LO - 1), LO))
    folded = lax.dot_general(
        masked_ref[...], jnp.concatenate(hots, axis=1), NT, preferred_element_type=F32
    )
    total = (grad_ref[...] + folded).astype(BF)
    for g in range(GROUPS):
        out_ref[g] = total[(g // 2) * C : (g // 2 + 1) * C, (g % 2) * CAP : (g % 2 + 1) * CAP]


def fold_faces(table_grad, from_low, from_high, face_rows):
    return pl.pallas_call(
        fold_kernel,
        out_shape=jax.ShapeDtypeStruct((GROUPS, C, CAP), BF),
        scratch_shapes=[pltpu.VMEM((BANKS * C, 2 * F), BF)],
        compiler_params=pltpu.CompilerParams(vmem_limit_bytes=48 << 20),
        name="fold",
    )(table_grad, from_low, from_high, face_rows)


def take_back_kernel(back_ref, owner_ref, slot_ref, out_ref):
    table = back_ref[...].reshape(GROUPS * C, CAP)
    for b in range(R // LO):
        cols = slice(b * LO, (b + 1) * LO)
        product = jnp.dot(table, onehot_rows(slot_ref[:, cols], CAP), preferred_element_type=F32)
        out_ref[:, cols] = select_banks(product, owner_ref[:, cols], GROUPS).astype(BF)


def take_back(returned, owner, slot):
    return pl.pallas_call(
        take_back_kernel,
        out_shape=jax.ShapeDtypeStruct((C, R), BF),
        compiler_params=pltpu.CompilerParams(vmem_limit_bytes=48 << 20),
        name="take_back",
    )(returned, owner, slot)


def unpack_kernel(scale, parts_ref, out_ref, flat_ref):
    for g in range(GROUPS):
        block = parts_ref[g] * scale
        for slot in range(SLOTS):
            i, t = divmod(g * SLOTS + slot, TILES)
            flat_ref[i * 8 : (i + 1) * 8, t * LANES : (t + 1) * LANES] = block[slot * 8 : (slot + 1) * 8, :]
        if g < C // 8:
            flat_ref[g * 8 : (g + 1) * 8, TILES * LANES :] = block[SLOTS * 8 :, :]
    for k in range(K):
        out_ref[k] = flat_ref[:, k * C : (k + 1) * C]


def unpack_weight(parts, scale):
    return pl.pallas_call(
        functools.partial(unpack_kernel, scale),
        out_shape=jax.ShapeDtypeStruct((K, C, C), F32),
        scratch_shapes=[pltpu.VMEM((C, (TILES + 1) * LANES), F32)],
        compiler_params=pltpu.CompilerParams(vmem_limit_bytes=32 << 20),
        name="unpack",
    )(parts)


def body(points, owners, kernel_maps, face_rows, weight, cotangent):
    points, owner = points[0, 0], owners.reshape(1, R)
    kernel_map, face_list, incoming = kernel_maps.reshape(K, 1, V), face_rows[0, 0], cotangent[0, 0]
    side = lax.axis_size("sy")
    up = [(i, i + 1) for i in range(side - 1)]
    down = [(i + 1, i) for i in range(side - 1)]

    outgoing, slot = place_points(points, owner)
    owned = lax.all_to_all(outgoing, "sx", 0, 0, tiled=True)
    lower, upper = take_faces(owned, face_list)
    ghost_low = lax.ppermute(upper, "sy", up)
    ghost_high = lax.ppermute(lower, "sy", down)
    weight_rows = jnp.transpose(weight, (1, 0, 2)).reshape(C, K * C)
    output, grad_pre, weight_part = forward_pass(
        owned, ghost_low, ghost_high, kernel_map, weight_rows, incoming
    )
    weight_columns = jnp.transpose(weight, (0, 2, 1)).reshape(K * C, C)
    scatter = functools.partial(scatter_part, kernel_map=kernel_map, weight=weight_columns, grad_pre=grad_pre)
    row_sum = lax.psum_scatter(weight_part, "sx", scatter_dimension=0, tiled=False)
    sums = scatter(0, grad_pre, grad_pre)
    share = lax.psum(row_sum, "sy")
    sums = scatter(1, row_sum, sums)
    parts = lax.all_gather(share, "sx", axis=0)
    table_grad, to_low, to_high = scatter(2, share, sums)
    from_low = lax.ppermute(to_high, "sy", up)
    from_high = lax.ppermute(to_low, "sy", down)
    owned_grad = fold_faces(table_grad, from_low, from_high, face_list)
    returned = lax.all_to_all(owned_grad, "sx", 0, 0, tiled=True)
    point_grad = take_back(returned, owner, slot)
    weight_grad = unpack_weight(parts, 1.0 / math.sqrt(GROUPS * side * V))
    return (output[None, None], point_grad[None, None], weight_grad)


def solution(mesh):
    split = P("sx", "sy", None, None)
    return jax.shard_map(
        body,
        mesh=mesh,
        in_specs=(split, split, split, split, P(), split),
        out_specs=(split, split, P()),
        check_vma=False,
    )
```

```python
import math

import jax
import jax.numpy as jnp
from jax import lax
from jax.experimental import pallas as pl
from jax.experimental.pallas import tpu as pltpu
from jax.sharding import PartitionSpec as P

C = 96
K = 27
R = 1024
F = 256
CAP = 128
V = 2048
GROUPS = 16
LO = 256
BANKS = V // LO
ALL_BANKS = BANKS + 2
WIDE = 512
WIDE_BANKS = ALL_BANKS * LO // WIDE
VB = 256
PER_DOT = 3

BF = jnp.bfloat16
F32 = jnp.float32
NT = (((1,), (1,)), ((), ()))


def rows16(index):
    return jnp.broadcast_to(index, (16, index.shape[-1])).astype(jnp.int16)


def onehot_rows(low, rows):
    n = low.shape[-1]
    row = lax.broadcasted_iota(jnp.int16, (rows, n), 0).reshape(rows // 16, 16, n)
    return jnp.where(row == rows16(low)[None], BF(1), BF(0)).reshape(rows, n)


def select_banks(product, bank, banks):
    n = bank.shape[-1]
    bank8 = jnp.broadcast_to(bank, (8, n))
    kept = jnp.zeros((C // 8, 8, n), F32)
    for a in range(banks):
        part = product[a * C : (a + 1) * C].reshape(C // 8, 8, n)
        kept = jnp.where((bank8 == a)[None], part, kept)
    return kept.reshape(C, n)


def masked_banks(values, bank, banks, out_ref, column):
    n = bank.shape[-1]
    bank16 = rows16(bank)
    values = values.reshape(C // 16, 16, n)
    for a in range(banks):
        spread = jnp.where((bank16 == a)[None], values, BF(0))
        out_ref[a * C : (a + 1) * C, column : column + n] = spread.reshape(C, n)


def place_kernel(points_ref, owner_ref, out_ref, slot_ref, masked_ref):
    owner = owner_ref[...]
    row = lax.broadcasted_iota(jnp.int32, (CAP, CAP), 0)
    col = lax.broadcasted_iota(jnp.int32, (CAP, CAP), 1)
    earlier = jnp.where(row < col, 1.0, 0.0).astype(BF)
    group = lax.broadcasted_iota(jnp.int32, (GROUPS, CAP), 0)
    total = jnp.zeros((GROUPS, 1), F32)
    for b in range(R // CAP):
        mine = jnp.where(group == owner[:, b * CAP : (b + 1) * CAP], 1.0, 0.0)
        before = jnp.dot(mine.astype(BF), earlier, preferred_element_type=F32) + total
        slot = jnp.sum(mine * before, axis=0, keepdims=True)
        slot_ref[:, b * CAP : (b + 1) * CAP] = slot.astype(jnp.int32)
        total = total + jnp.sum(mine, axis=1, keepdims=True)
    masked_banks(points_ref[...], owner, GROUPS, masked_ref, 0)
    onehot = onehot_rows(slot_ref[...], CAP)
    for g in range(GROUPS):
        out_ref[g] = lax.dot_general(
            masked_ref[g * C : (g + 1) * C, :], onehot, NT, preferred_element_type=F32
        ).astype(BF)


def place_points(points, owner):
    return pl.pallas_call(
        place_kernel,
        out_shape=(
            jax.ShapeDtypeStruct((GROUPS, C, CAP), BF),
            jax.ShapeDtypeStruct((1, R), jnp.int32),
        ),
        scratch_shapes=[pltpu.VMEM((GROUPS * C, R), BF)],
        compiler_params=pltpu.CompilerParams(vmem_limit_bytes=16 << 20),
        name="place",
    )(points, owner)


def faces_kernel(owned_ref, rows_ref, lower_ref, upper_ref):
    table = owned_ref[...].reshape(GROUPS * C, CAP)
    for j, out_ref in enumerate((lower_ref, upper_ref)):
        rows = rows_ref[j : j + 1, :]
        product = jnp.dot(table, onehot_rows(rows & (CAP - 1), CAP), preferred_element_type=F32)
        out_ref[...] = select_banks(product, rows >> 7, GROUPS).astype(BF)


def take_faces(owned, face_rows):
    return pl.pallas_call(
        faces_kernel,
        out_shape=(jax.ShapeDtypeStruct((C, F), BF),) * 2,
        compiler_params=pltpu.CompilerParams(vmem_limit_bytes=16 << 20),
        name="faces",
    )(owned, face_rows)


def forward_kernel(
    owned_ref, low_ref, high_ref, map_ref, weight_ref, cot_ref, out_ref, pre_ref, wg_ref, table_ref, picked_ref, acc_ref
):
    step = pl.program_id(0)

    @pl.when(step == 0)
    def _():
        per = WIDE // CAP
        for g in range(GROUPS):
            table_ref[(g // per) * C : (g // per + 1) * C, (g % per) * CAP : (g % per + 1) * CAP] = owned_ref[g]
        table_ref[(WIDE_BANKS - 1) * C :, :F] = low_ref[...]
        table_ref[(WIDE_BANKS - 1) * C :, F:] = high_ref[...]
        acc_ref[...] = jnp.zeros_like(acc_ref)

    table = table_ref[...]
    for k in range(K):
        index = map_ref[k]
        product = jnp.dot(table, onehot_rows(index & (WIDE - 1), WIDE), preferred_element_type=F32)
        picked_ref[k * C : (k + 1) * C, :] = select_banks(product, index >> 9, WIDE_BANKS).astype(BF)
    preact = jnp.dot(weight_ref[...], picked_ref[...], preferred_element_type=F32)
    logistic = jax.nn.sigmoid(preact)
    out_ref[...] = (preact * logistic).astype(BF)
    slope = logistic * (1.0 + preact * (1.0 - logistic))
    grad_pre = (cot_ref[...].astype(F32) * slope).astype(BF)
    pre_ref[...] = grad_pre
    acc_ref[...] += lax.dot_general(picked_ref[...], grad_pre, NT, preferred_element_type=F32)

    @pl.when(step == pl.num_programs(0) - 1)
    def _():
        for k in range(K):
            wg_ref[k] = acc_ref[k * C : (k + 1) * C, :].T


def forward_pass(owned, low, high, kernel_map, weight, cotangent):
    whole = lambda *shape: pl.BlockSpec(shape, lambda i: (0,) * len(shape))
    column = lambda rows: pl.BlockSpec((rows, VB), lambda i: (0, i))
    return pl.pallas_call(
        forward_kernel,
        grid=(V // VB,),
        in_specs=[
            whole(GROUPS, C, CAP),
            whole(C, F),
            whole(C, F),
            pl.BlockSpec((K, 1, VB), lambda i: (0, 0, i)),
            whole(C, K * C),
            column(C),
        ],
        out_specs=(column(C), column(C), whole(K, C, C)),
        out_shape=(
            jax.ShapeDtypeStruct((C, V), BF),
            jax.ShapeDtypeStruct((C, V), BF),
            jax.ShapeDtypeStruct((K, C, C), F32),
        ),
        scratch_shapes=[
            pltpu.VMEM((WIDE_BANKS * C, WIDE), BF),
            pltpu.VMEM((K * C, VB), BF),
            pltpu.VMEM((K * C, C), F32),
        ],
        compiler_params=pltpu.CompilerParams(vmem_limit_bytes=20 << 20),
        cost_estimate=pl.CostEstimate(
            flops=2 * K * V * ALL_BANKS * C * LO, bytes_accessed=4 << 20, transcendentals=C * V
        ),
        name="gather_forward",
    )(owned, low, high, kernel_map, weight, cotangent)


def scatter_step(map_ref, weight_ref, pre_ref, acc_ref, spread_ref, masked_ref):
    spread_ref[...] = jnp.dot(weight_ref[...], pre_ref[...], preferred_element_type=F32).astype(BF)
    for first in range(0, K, PER_DOT):
        hots = []
        for j in range(PER_DOT):
            k = first + j
            index = map_ref[k]
            masked_banks(spread_ref[k * C : (k + 1) * C, :], index >> 8, ALL_BANKS, masked_ref, j * VB)
            hots.append(onehot_rows(index & (LO - 1), LO))
        acc_ref[...] += lax.dot_general(
            masked_ref[...], jnp.concatenate(hots, axis=1), NT, preferred_element_type=F32
        )


def scatter_kernel(map_ref, weight_ref, pre_ref, own_ref, low_ref, high_ref, spread_ref, masked_ref, acc_ref):
    @pl.when(pl.program_id(0) == 0)
    def _():
        acc_ref[...] = jnp.zeros_like(acc_ref)

    scatter_step(map_ref, weight_ref, pre_ref, acc_ref, spread_ref, masked_ref)

    @pl.when(pl.program_id(0) == pl.num_programs(0) - 1)
    def _():
        own_ref[...] = acc_ref[: BANKS * C, :]
        low_ref[...] = acc_ref[BANKS * C : (BANKS + 1) * C, :].astype(BF)
        high_ref[...] = acc_ref[(BANKS + 1) * C :, :].astype(BF)


def scatter_pass(kernel_map, weight, grad_pre):
    whole = lambda *shape: pl.BlockSpec(shape, lambda i: (0,) * len(shape))
    return pl.pallas_call(
        scatter_kernel,
        grid=(V // VB,),
        in_specs=[
            pl.BlockSpec((K, 1, VB), lambda i: (0, 0, i)),
            whole(K * C, C),
            pl.BlockSpec((C, VB), lambda i: (0, i)),
        ],
        out_specs=(whole(BANKS * C, LO), whole(C, F), whole(C, F)),
        out_shape=(
            jax.ShapeDtypeStruct((BANKS * C, LO), F32),
            jax.ShapeDtypeStruct((C, F), BF),
            jax.ShapeDtypeStruct((C, F), BF),
        ),
        scratch_shapes=[
            pltpu.VMEM((K * C, VB), BF),
            pltpu.VMEM((ALL_BANKS * C, PER_DOT * VB), BF),
            pltpu.VMEM((ALL_BANKS * C, LO), F32),
        ],
        compiler_params=pltpu.CompilerParams(vmem_limit_bytes=20 << 20),
        cost_estimate=pl.CostEstimate(
            flops=2 * K * V * ALL_BANKS * C * LO, bytes_accessed=2 << 20, transcendentals=0
        ),
        name="scatter",
    )(kernel_map, weight, grad_pre)


def fold_kernel(grad_ref, from_low_ref, from_high_ref, rows_ref, out_ref, masked_ref):
    hots = []
    for j, part_ref in enumerate((from_low_ref, from_high_ref)):
        rows = rows_ref[j : j + 1, :]
        masked_banks(part_ref[...], rows >> 8, BANKS, masked_ref, j * F)
        hots.append(onehot_rows(rows & (LO - 1), LO))
    folded = lax.dot_general(
        masked_ref[...], jnp.concatenate(hots, axis=1), NT, preferred_element_type=F32
    )
    total = (grad_ref[...] + folded).astype(BF)
    for g in range(GROUPS):
        out_ref[g] = total[(g // 2) * C : (g // 2 + 1) * C, (g % 2) * CAP : (g % 2 + 1) * CAP]


def fold_faces(table_grad, from_low, from_high, face_rows):
    return pl.pallas_call(
        fold_kernel,
        out_shape=jax.ShapeDtypeStruct((GROUPS, C, CAP), BF),
        scratch_shapes=[pltpu.VMEM((BANKS * C, 2 * F), BF)],
        compiler_params=pltpu.CompilerParams(vmem_limit_bytes=16 << 20),
        name="fold",
    )(table_grad, from_low, from_high, face_rows)


def take_back_kernel(back_ref, owner_ref, slot_ref, out_ref):
    table = back_ref[...].reshape(GROUPS * C, CAP)
    for b in range(R // LO):
        cols = slice(b * LO, (b + 1) * LO)
        product = jnp.dot(table, onehot_rows(slot_ref[:, cols], CAP), preferred_element_type=F32)
        out_ref[:, cols] = select_banks(product, owner_ref[:, cols], GROUPS).astype(BF)


def take_back(returned, owner, slot):
    return pl.pallas_call(
        take_back_kernel,
        out_shape=jax.ShapeDtypeStruct((C, R), BF),
        compiler_params=pltpu.CompilerParams(vmem_limit_bytes=16 << 20),
        name="take_back",
    )(returned, owner, slot)


def body(points, owners, kernel_maps, face_rows, weight, cotangent):
    points, owner = points[0, 0], owners.reshape(1, R)
    kernel_map, face_list, incoming = kernel_maps.reshape(K, 1, V), face_rows[0, 0], cotangent[0, 0]
    side = lax.axis_size("sy")
    up = [(i, i + 1) for i in range(side - 1)]
    down = [(i + 1, i) for i in range(side - 1)]

    outgoing, slot = place_points(points, owner)
    owned = lax.all_to_all(outgoing, "sx", 0, 0, tiled=True)
    lower, upper = take_faces(owned, face_list)
    ghost_low = lax.ppermute(upper, "sy", up)
    ghost_high = lax.ppermute(lower, "sy", down)
    weight_rows = jnp.transpose(weight, (1, 0, 2)).reshape(C, K * C)
    output, grad_pre, weight_part = forward_pass(
        owned, ghost_low, ghost_high, kernel_map, weight_rows, incoming
    )
    weight_columns = jnp.transpose(weight, (0, 2, 1)).reshape(K * C, C)
    table_grad, to_low, to_high = scatter_pass(kernel_map, weight_columns, grad_pre)
    from_low = lax.ppermute(to_high, "sy", up)
    from_high = lax.ppermute(to_low, "sy", down)
    owned_grad = fold_faces(table_grad, from_low, from_high, face_list)
    returned = lax.all_to_all(owned_grad, "sx", 0, 0, tiled=True)
    point_grad = take_back(returned, owner, slot)
    weight_sum = lax.psum(weight_part, ("sx", "sy")).astype(BF)
    weight_grad = weight_sum.astype(F32) * (1.0 / math.sqrt(GROUPS * side * V))
    return (output[None, None], point_grad[None, None], weight_grad)


def solution(mesh):
    split = P("sx", "sy", None, None)
    return jax.shard_map(
        body,
        mesh=mesh,
        in_specs=(split, split, split, split, P(), split),
        out_specs=(split, split, P()),
        check_vma=False,
    )
```

```python
import functools
import math

import jax
import jax.numpy as jnp
from jax import lax
from jax.experimental import pallas as pl
from jax.experimental.pallas import tpu as pltpu
from jax.sharding import PartitionSpec as P

C = 96
K = 27
R = 1024
F = 256
CAP = 128
V = 2048
GROUPS = 16
LO = 256
BANKS = V // LO
ALL_BANKS = BANKS + 2
WIDE = 512
WIDE_BANKS = ALL_BANKS * LO // WIDE
VB = 256
FORWARD_VB = 512
PER_DOT = 3
PARTS = (3, 3, 2)
LANES = 128
TILES = K * C // LANES
SHARD_TILES = 8

BF = jnp.bfloat16
F32 = jnp.float32
NT = (((1,), (1,)), ((), ()))


def rows16(index):
    return jnp.broadcast_to(index, (16, index.shape[-1])).astype(jnp.int16)


def onehot_rows(low, rows):
    n = low.shape[-1]
    row = lax.broadcasted_iota(jnp.int16, (rows, n), 0).reshape(rows // 16, 16, n)
    return jnp.where(row == rows16(low)[None], BF(1), BF(0)).reshape(rows, n)


def select_banks(product, bank, banks):
    n = bank.shape[-1]
    bank8 = jnp.broadcast_to(bank, (8, n))
    kept = jnp.zeros((C // 8, 8, n), F32)
    for a in range(banks):
        part = product[a * C : (a + 1) * C].reshape(C // 8, 8, n)
        kept = jnp.where((bank8 == a)[None], part, kept)
    return kept.reshape(C, n)


def masked_banks(values, bank, banks, out_ref, column):
    n = bank.shape[-1]
    bank16 = rows16(bank)
    values = values.reshape(C // 16, 16, n)
    for a in range(banks):
        spread = jnp.where((bank16 == a)[None], values, BF(0))
        out_ref[a * C : (a + 1) * C, column : column + n] = spread.reshape(C, n)


def tile_place(i, t):
    return divmod(i * TILES + t if t < TILES else (C // 16) * TILES + i, SHARD_TILES)


def place_kernel(points_ref, owner_ref, out_ref, slot_ref, masked_ref):
    owner = owner_ref[...]
    row = lax.broadcasted_iota(jnp.int32, (CAP, CAP), 0)
    col = lax.broadcasted_iota(jnp.int32, (CAP, CAP), 1)
    earlier = jnp.where(row < col, 1.0, 0.0).astype(BF)
    group = lax.broadcasted_iota(jnp.int32, (GROUPS, CAP), 0)
    total = jnp.zeros((GROUPS, 1), F32)
    for b in range(R // CAP):
        mine = jnp.where(group == owner[:, b * CAP : (b + 1) * CAP], 1.0, 0.0)
        before = jnp.dot(mine.astype(BF), earlier, preferred_element_type=F32) + total
        slot = jnp.sum(mine * before, axis=0, keepdims=True)
        slot_ref[:, b * CAP : (b + 1) * CAP] = slot.astype(jnp.int32)
        total = total + jnp.sum(mine, axis=1, keepdims=True)
    masked_banks(points_ref[...], owner, GROUPS, masked_ref, 0)
    onehot = onehot_rows(slot_ref[...], CAP)
    for g in range(GROUPS):
        out_ref[g] = lax.dot_general(
            masked_ref[g * C : (g + 1) * C, :], onehot, NT, preferred_element_type=F32
        ).astype(BF)


def place_points(points, owner):
    return pl.pallas_call(
        place_kernel,
        out_shape=(
            jax.ShapeDtypeStruct((GROUPS, C, CAP), BF),
            jax.ShapeDtypeStruct((1, R), jnp.int32),
        ),
        scratch_shapes=[pltpu.VMEM((GROUPS * C, R), BF)],
        compiler_params=pltpu.CompilerParams(vmem_limit_bytes=16 << 20),
        name="place",
    )(points, owner)


def faces_kernel(owned_ref, rows_ref, lower_ref, upper_ref):
    table = owned_ref[...].reshape(GROUPS * C, CAP)
    for j, out_ref in enumerate((lower_ref, upper_ref)):
        rows = rows_ref[j : j + 1, :]
        product = jnp.dot(table, onehot_rows(rows & (CAP - 1), CAP), preferred_element_type=F32)
        out_ref[...] = select_banks(product, rows >> 7, GROUPS).astype(BF)


def take_faces(owned, face_rows):
    return pl.pallas_call(
        faces_kernel,
        out_shape=(jax.ShapeDtypeStruct((C, F), BF),) * 2,
        compiler_params=pltpu.CompilerParams(vmem_limit_bytes=16 << 20),
        name="faces",
    )(owned, face_rows)


def forward_kernel(
    owned_ref, low_ref, high_ref, map_ref, weight_ref, cot_ref, out_ref, pre_ref, wg_ref, table_ref, picked_ref, acc_ref
):
    step = pl.program_id(0)

    @pl.when(step == 0)
    def _():
        per = WIDE // CAP
        for g in range(GROUPS):
            table_ref[(g // per) * C : (g // per + 1) * C, (g % per) * CAP : (g % per + 1) * CAP] = owned_ref[g]
        table_ref[(WIDE_BANKS - 1) * C :, :F] = low_ref[...]
        table_ref[(WIDE_BANKS - 1) * C :, F:] = high_ref[...]
        acc_ref[...] = jnp.zeros_like(acc_ref)

    table = table_ref[...]
    for k in range(K):
        index = map_ref[k]
        product = jnp.dot(table, onehot_rows(index & (WIDE - 1), WIDE), preferred_element_type=F32)
        picked_ref[k * C : (k + 1) * C, :] = select_banks(product, index >> 9, WIDE_BANKS).astype(BF)
    preact = jnp.dot(weight_ref[...], picked_ref[...], preferred_element_type=F32)
    logistic = jax.nn.sigmoid(preact)
    out_ref[...] = (preact * logistic).astype(BF)
    slope = logistic * (1.0 + preact * (1.0 - logistic))
    grad_pre = (cot_ref[...].astype(F32) * slope).astype(BF)
    pre_ref[...] = grad_pre
    acc_ref[...] += lax.dot_general(picked_ref[...], grad_pre, NT, preferred_element_type=F32)

    @pl.when(step == pl.num_programs(0) - 1)
    def _():
        for t in range(TILES + 1):
            block = acc_ref[t * LANES : min((t + 1) * LANES, K * C), :].T
            if t == TILES:
                block = jnp.concatenate([block, jnp.zeros((C, LANES - block.shape[1]), F32)], axis=1)
            block = block.astype(BF)
            for i in range(C // 16):
                shard, slot = tile_place(i, t)
                wg_ref[shard, slot * 16 : (slot + 1) * 16, :] = block[i * 16 : (i + 1) * 16, :]
        used = (TILES + 1) * (C // 16) - (GROUPS - 1) * SHARD_TILES
        wg_ref[GROUPS - 1, used * 16 :, :] = jnp.zeros((LANES - used * 16, LANES), BF)


def forward_pass(owned, low, high, kernel_map, weight, cotangent):
    whole = lambda *shape: pl.BlockSpec(shape, lambda i: (0,) * len(shape))
    column = lambda rows: pl.BlockSpec((rows, FORWARD_VB), lambda i: (0, i))
    return pl.pallas_call(
        forward_kernel,
        grid=(V // FORWARD_VB,),
        in_specs=[
            whole(GROUPS, C, CAP),
            whole(C, F),
            whole(C, F),
            pl.BlockSpec((K, 1, FORWARD_VB), lambda i: (0, 0, i)),
            whole(C, K * C),
            column(C),
        ],
        out_specs=(column(C), column(C), whole(GROUPS, LANES, LANES)),
        out_shape=(
            jax.ShapeDtypeStruct((C, V), BF),
            jax.ShapeDtypeStruct((C, V), BF),
            jax.ShapeDtypeStruct((GROUPS, LANES, LANES), BF),
        ),
        scratch_shapes=[
            pltpu.VMEM((WIDE_BANKS * C, WIDE), BF),
            pltpu.VMEM((K * C, FORWARD_VB), BF),
            pltpu.VMEM((K * C, C), F32),
        ],
        compiler_params=pltpu.CompilerParams(vmem_limit_bytes=32 << 20),
        cost_estimate=pl.CostEstimate(
            flops=2 * K * V * ALL_BANKS * C * LO, bytes_accessed=4 << 20, transcendentals=C * V
        ),
        name="gather_forward",
    )(owned, low, high, kernel_map, weight, cotangent)


def scatter_step(map_ref, weight_ref, pre_ref, acc_ref, spread_ref, masked_ref):
    spread_ref[...] = jnp.dot(weight_ref[...], pre_ref[...], preferred_element_type=F32).astype(BF)
    for turn in range(K // PER_DOT):
        hots = []
        slot = masked_ref.at[turn % 2]
        for j in range(PER_DOT):
            k = turn * PER_DOT + j
            index = map_ref[k]
            masked_banks(spread_ref[k * C : (k + 1) * C, :], index >> 8, ALL_BANKS, slot, j * VB)
            hots.append(onehot_rows(index & (LO - 1), LO))
        acc_ref[...] += lax.dot_general(
            slot[...], jnp.concatenate(hots, axis=1), NT, preferred_element_type=F32
        )


def scatter_kernel(has_start, has_faces, after_ref, start_ref, map_ref, weight_ref, pre_ref, *refs):
    if has_faces:
        own_ref, low_ref, high_ref, spread_ref, masked_ref, acc_ref = refs
    else:
        acc_ref, spread_ref, masked_ref = refs

    @pl.when(pl.program_id(0) == 0)
    def _():
        acc_ref[...] = start_ref[...] if has_start else jnp.zeros_like(acc_ref)

    scatter_step(map_ref, weight_ref, pre_ref, acc_ref, spread_ref, masked_ref)

    if has_faces:

        @pl.when(pl.program_id(0) == pl.num_programs(0) - 1)
        def _():
            own_ref[...] = acc_ref[: BANKS * C, :]
            low_ref[...] = acc_ref[BANKS * C : (BANKS + 1) * C, :].astype(BF)
            high_ref[...] = acc_ref[(BANKS + 1) * C :, :].astype(BF)


def scatter_part(part, after, start, kernel_map, weight, grad_pre):
    whole = lambda *shape: pl.BlockSpec(shape, lambda i: (0,) * len(shape))
    sums = jax.ShapeDtypeStruct((ALL_BANKS * C, LO), F32)
    scratch = [pltpu.VMEM((K * C, VB), BF), pltpu.VMEM((2, ALL_BANKS * C, PER_DOT * VB), BF)]
    at, steps, last = sum(PARTS[:part]), PARTS[part], part == len(PARTS) - 1
    if last:
        out_specs = (whole(BANKS * C, LO), whole(C, F), whole(C, F))
        out_shape = (
            jax.ShapeDtypeStruct((BANKS * C, LO), F32),
            jax.ShapeDtypeStruct((C, F), BF),
            jax.ShapeDtypeStruct((C, F), BF),
        )
        scratch.append(pltpu.VMEM(sums.shape, F32))
    else:
        out_specs, out_shape = whole(*sums.shape), sums
    return pl.pallas_call(
        functools.partial(scatter_kernel, part > 0, last),
        grid=(steps,),
        in_specs=[
            pl.BlockSpec(memory_space=pl.ANY),
            whole(*sums.shape) if part > 0 else pl.BlockSpec(memory_space=pl.ANY),
            pl.BlockSpec((K, 1, VB), lambda i: (0, 0, at + i)),
            whole(K * C, C),
            pl.BlockSpec((C, VB), lambda i: (0, at + i)),
        ],
        out_specs=out_specs,
        out_shape=out_shape,
        scratch_shapes=scratch,
        compiler_params=pltpu.CompilerParams(vmem_limit_bytes=24 << 20),
        cost_estimate=pl.CostEstimate(
            flops=2 * K * VB * steps * ALL_BANKS * C * LO, bytes_accessed=2 << 20, transcendentals=0
        ),
        name="scatter",
    )(after, start, kernel_map, weight, grad_pre)


def sum_parts_kernel(parts_ref, out_ref):
    total = parts_ref[0].astype(F32)
    for g in range(1, GROUPS):
        total = total + parts_ref[g].astype(F32)
    total = total.astype(BF)
    for g in range(GROUPS):
        out_ref[g] = total


def sum_parts(parts):
    return pl.pallas_call(
        sum_parts_kernel,
        out_shape=jax.ShapeDtypeStruct(parts.shape, BF),
        compiler_params=pltpu.CompilerParams(vmem_limit_bytes=8 << 20),
        name="sum_parts",
    )(parts)


def unpack_kernel(scale, parts_ref, out_ref, flat_ref):
    for t in range(TILES + 1):
        for i in range(C // 16):
            shard, slot = tile_place(i, t)
            tile = parts_ref[shard, slot * 16 : (slot + 1) * 16, :].astype(F32) * scale
            flat_ref[i * 16 : (i + 1) * 16, t * LANES : (t + 1) * LANES] = tile
    for k in range(K):
        out_ref[k] = flat_ref[:, k * C : (k + 1) * C]


def unpack_weight(parts, scale):
    return pl.pallas_call(
        functools.partial(unpack_kernel, scale),
        out_shape=jax.ShapeDtypeStruct((K, C, C), F32),
        scratch_shapes=[pltpu.VMEM((C, (TILES + 1) * LANES), F32)],
        compiler_params=pltpu.CompilerParams(vmem_limit_bytes=16 << 20),
        name="unpack",
    )(parts)


def fold_kernel(grad_ref, from_low_ref, from_high_ref, rows_ref, out_ref, masked_ref):
    hots = []
    for j, part_ref in enumerate((from_low_ref, from_high_ref)):
        rows = rows_ref[j : j + 1, :]
        masked_banks(part_ref[...], rows >> 8, BANKS, masked_ref, j * F)
        hots.append(onehot_rows(rows & (LO - 1), LO))
    folded = lax.dot_general(
        masked_ref[...], jnp.concatenate(hots, axis=1), NT, preferred_element_type=F32
    )
    total = (grad_ref[...] + folded).astype(BF)
    for g in range(GROUPS):
        out_ref[g] = total[(g // 2) * C : (g // 2 + 1) * C, (g % 2) * CAP : (g % 2 + 1) * CAP]


def fold_faces(table_grad, from_low, from_high, face_rows):
    return pl.pallas_call(
        fold_kernel,
        out_shape=jax.ShapeDtypeStruct((GROUPS, C, CAP), BF),
        scratch_shapes=[pltpu.VMEM((BANKS * C, 2 * F), BF)],
        compiler_params=pltpu.CompilerParams(vmem_limit_bytes=16 << 20),
        name="fold",
    )(table_grad, from_low, from_high, face_rows)


def take_back_kernel(back_ref, owner_ref, slot_ref, out_ref):
    table = back_ref[...].reshape(GROUPS * C, CAP)
    for b in range(R // LO):
        cols = slice(b * LO, (b + 1) * LO)
        product = jnp.dot(table, onehot_rows(slot_ref[:, cols], CAP), preferred_element_type=F32)
        out_ref[:, cols] = select_banks(product, owner_ref[:, cols], GROUPS).astype(BF)


def take_back(returned, owner, slot):
    return pl.pallas_call(
        take_back_kernel,
        out_shape=jax.ShapeDtypeStruct((C, R), BF),
        compiler_params=pltpu.CompilerParams(vmem_limit_bytes=16 << 20),
        name="take_back",
    )(returned, owner, slot)


def body(points, owners, kernel_maps, face_rows, weight, cotangent):
    points, owner = points[0, 0], owners.reshape(1, R)
    kernel_map, face_list, incoming = kernel_maps.reshape(K, 1, V), face_rows[0, 0], cotangent[0, 0]
    side = lax.axis_size("sy")
    up = [(i, i + 1) for i in range(side - 1)]
    down = [(i + 1, i) for i in range(side - 1)]

    outgoing, slot = place_points(points, owner)
    owned = lax.all_to_all(outgoing, "sx", 0, 0, tiled=True)
    lower, upper = take_faces(owned, face_list)
    ghost_low = lax.ppermute(upper, "sy", up)
    ghost_high = lax.ppermute(lower, "sy", down)
    weight_rows = jnp.transpose(weight, (1, 0, 2)).reshape(C, K * C)
    output, grad_pre, weight_part = forward_pass(
        owned, ghost_low, ghost_high, kernel_map, weight_rows, incoming
    )
    weight_columns = jnp.transpose(weight, (0, 2, 1)).reshape(K * C, C)
    scatter = functools.partial(scatter_part, kernel_map=kernel_map, weight=weight_columns, grad_pre=grad_pre)
    across = lambda array, axis: lax.all_to_all(array, axis, 0, 0, tiled=True)
    row_sums = sum_parts(across(weight_part, "sx"))
    sums = scatter(0, grad_pre, grad_pre)
    all_sums = sum_parts(across(row_sums, "sy"))
    sums = scatter(1, row_sums, sums)
    parts = across(all_sums, "sx")
    table_grad, to_low, to_high = scatter(2, all_sums, sums)
    from_low = lax.ppermute(to_high, "sy", up)
    from_high = lax.ppermute(to_low, "sy", down)
    owned_grad = fold_faces(table_grad, from_low, from_high, face_list)
    returned = lax.all_to_all(owned_grad, "sx", 0, 0, tiled=True)
    point_grad = take_back(returned, owner, slot)
    weight_grad = unpack_weight(parts, 1.0 / math.sqrt(GROUPS * side * V))
    return (output[None, None], point_grad[None, None], weight_grad)


def solution(mesh):
    split = P("sx", "sy", None, None)
    return jax.shard_map(
        body,
        mesh=mesh,
        in_specs=(split, split, split, split, P(), split),
        out_specs=(split, split, P()),
        check_vma=False,
    )
```

```python
import functools
import math

import jax
import jax.numpy as jnp
from jax import lax
from jax.experimental import pallas as pl
from jax.experimental.pallas import tpu as pltpu
from jax.sharding import PartitionSpec as P

C = 96
K = 27
R = 1024
F = 256
CAP = 128
V = 2048
GROUPS = 16
LO = 256
BANKS = V // LO
ALL_BANKS = BANKS + 2
WIDE = 512
WIDE_BANKS = ALL_BANKS * LO // WIDE
VB = 512
FORWARD_VB = 1024
PER_DOT = 3
PARTS = (2, 1, 1)
LANES = 128
TILES = K * C // LANES
SHARD_TILES = 8

BF = jnp.bfloat16
F32 = jnp.float32
NT = (((1,), (1,)), ((), ()))


def rows16(index):
    return jnp.broadcast_to(index, (16, index.shape[-1])).astype(jnp.int16)


def onehot_rows(low, rows):
    n = low.shape[-1]
    row = lax.broadcasted_iota(jnp.int16, (rows, n), 0).reshape(rows // 16, 16, n)
    return jnp.where(row == rows16(low)[None], BF(1), BF(0)).reshape(rows, n)


def select_banks(product, bank, banks):
    n = bank.shape[-1]
    bank8 = jnp.broadcast_to(bank, (8, n))
    kept = jnp.zeros((C // 8, 8, n), F32)
    for a in range(banks):
        part = product[a * C : (a + 1) * C].reshape(C // 8, 8, n)
        kept = jnp.where((bank8 == a)[None], part, kept)
    return kept.reshape(C, n)


def masked_banks(values, bank, banks, out_ref, column):
    n = bank.shape[-1]
    bank16 = rows16(bank)
    values = values.reshape(C // 16, 16, n)
    for a in range(banks):
        spread = jnp.where((bank16 == a)[None], values, BF(0))
        out_ref[a * C : (a + 1) * C, column : column + n] = spread.reshape(C, n)


def tile_place(i, t):
    return divmod(i * TILES + t if t < TILES else (C // 16) * TILES + i, SHARD_TILES)


def place_kernel(points_ref, owner_ref, out_ref, slot_ref, masked_ref):
    owner = owner_ref[...]
    row = lax.broadcasted_iota(jnp.int32, (CAP, CAP), 0)
    col = lax.broadcasted_iota(jnp.int32, (CAP, CAP), 1)
    earlier = jnp.where(row < col, 1.0, 0.0).astype(BF)
    group = lax.broadcasted_iota(jnp.int32, (GROUPS, CAP), 0)
    total = jnp.zeros((GROUPS, 1), F32)
    for b in range(R // CAP):
        mine = jnp.where(group == owner[:, b * CAP : (b + 1) * CAP], 1.0, 0.0)
        before = jnp.dot(mine.astype(BF), earlier, preferred_element_type=F32) + total
        slot = jnp.sum(mine * before, axis=0, keepdims=True)
        slot_ref[:, b * CAP : (b + 1) * CAP] = slot.astype(jnp.int32)
        total = total + jnp.sum(mine, axis=1, keepdims=True)
    masked_banks(points_ref[...], owner, GROUPS, masked_ref, 0)
    onehot = onehot_rows(slot_ref[...], CAP)
    for g in range(GROUPS):
        out_ref[g] = lax.dot_general(
            masked_ref[g * C : (g + 1) * C, :], onehot, NT, preferred_element_type=F32
        ).astype(BF)


def place_points(points, owner):
    return pl.pallas_call(
        place_kernel,
        out_shape=(
            jax.ShapeDtypeStruct((GROUPS, C, CAP), BF),
            jax.ShapeDtypeStruct((1, R), jnp.int32),
        ),
        scratch_shapes=[pltpu.VMEM((GROUPS * C, R), BF)],
        compiler_params=pltpu.CompilerParams(vmem_limit_bytes=16 << 20),
        name="place",
    )(points, owner)


def faces_kernel(owned_ref, rows_ref, lower_ref, upper_ref):
    table = owned_ref[...].reshape(GROUPS * C, CAP)
    for j, out_ref in enumerate((lower_ref, upper_ref)):
        rows = rows_ref[j : j + 1, :]
        product = jnp.dot(table, onehot_rows(rows & (CAP - 1), CAP), preferred_element_type=F32)
        out_ref[...] = select_banks(product, rows >> 7, GROUPS).astype(BF)


def take_faces(owned, face_rows):
    return pl.pallas_call(
        faces_kernel,
        out_shape=(jax.ShapeDtypeStruct((C, F), BF),) * 2,
        compiler_params=pltpu.CompilerParams(vmem_limit_bytes=16 << 20),
        name="faces",
    )(owned, face_rows)


def forward_kernel(
    owned_ref, low_ref, high_ref, map_ref, weight_ref, cot_ref, out_ref, pre_ref, wg_ref, table_ref, picked_ref, acc_ref
):
    step = pl.program_id(0)

    @pl.when(step == 0)
    def _():
        per = WIDE // CAP
        for g in range(GROUPS):
            table_ref[(g // per) * C : (g // per + 1) * C, (g % per) * CAP : (g % per + 1) * CAP] = owned_ref[g]
        table_ref[(WIDE_BANKS - 1) * C :, :F] = low_ref[...]
        table_ref[(WIDE_BANKS - 1) * C :, F:] = high_ref[...]
        acc_ref[...] = jnp.zeros_like(acc_ref)

    table = table_ref[...]
    for k in range(K):
        index = map_ref[k]
        product = jnp.dot(table, onehot_rows(index & (WIDE - 1), WIDE), preferred_element_type=F32)
        picked_ref[k * C : (k + 1) * C, :] = select_banks(product, index >> 9, WIDE_BANKS).astype(BF)
    preact = jnp.dot(weight_ref[...], picked_ref[...], preferred_element_type=F32)
    logistic = jax.nn.sigmoid(preact)
    out_ref[...] = (preact * logistic).astype(BF)
    slope = logistic * (1.0 + preact * (1.0 - logistic))
    grad_pre = (cot_ref[...].astype(F32) * slope).astype(BF)
    pre_ref[...] = grad_pre
    acc_ref[...] += lax.dot_general(picked_ref[...], grad_pre, NT, preferred_element_type=F32)

    @pl.when(step == pl.num_programs(0) - 1)
    def _():
        for t in range(TILES + 1):
            block = acc_ref[t * LANES : min((t + 1) * LANES, K * C), :].T
            if t == TILES:
                block = jnp.concatenate([block, jnp.zeros((C, LANES - block.shape[1]), F32)], axis=1)
            block = block.astype(BF)
            for i in range(C // 16):
                shard, slot = tile_place(i, t)
                wg_ref[shard, slot * 16 : (slot + 1) * 16, :] = block[i * 16 : (i + 1) * 16, :]
        used = (TILES + 1) * (C // 16) - (GROUPS - 1) * SHARD_TILES
        wg_ref[GROUPS - 1, used * 16 :, :] = jnp.zeros((LANES - used * 16, LANES), BF)


def forward_pass(owned, low, high, kernel_map, weight, cotangent):
    whole = lambda *shape: pl.BlockSpec(shape, lambda i: (0,) * len(shape))
    column = lambda rows: pl.BlockSpec((rows, FORWARD_VB), lambda i: (0, i))
    return pl.pallas_call(
        forward_kernel,
        grid=(V // FORWARD_VB,),
        in_specs=[
            whole(GROUPS, C, CAP),
            whole(C, F),
            whole(C, F),
            pl.BlockSpec((K, 1, FORWARD_VB), lambda i: (0, 0, i)),
            whole(C, K * C),
            column(C),
        ],
        out_specs=(column(C), column(C), whole(GROUPS, LANES, LANES)),
        out_shape=(
            jax.ShapeDtypeStruct((C, V), BF),
            jax.ShapeDtypeStruct((C, V), BF),
            jax.ShapeDtypeStruct((GROUPS, LANES, LANES), BF),
        ),
        scratch_shapes=[
            pltpu.VMEM((WIDE_BANKS * C, WIDE), BF),
            pltpu.VMEM((K * C, FORWARD_VB), BF),
            pltpu.VMEM((K * C, C), F32),
        ],
        compiler_params=pltpu.CompilerParams(vmem_limit_bytes=32 << 20),
        cost_estimate=pl.CostEstimate(
            flops=2 * K * V * ALL_BANKS * C * LO, bytes_accessed=4 << 20, transcendentals=C * V
        ),
        name="gather_forward",
    )(owned, low, high, kernel_map, weight, cotangent)


def scatter_step(map_ref, weight_ref, pre_ref, acc_ref, spread_ref, masked_ref):
    spread_ref[...] = jnp.dot(weight_ref[...], pre_ref[...], preferred_element_type=F32).astype(BF)
    for turn in range(K // PER_DOT):
        hots = []
        slot = masked_ref.at[turn % 2]
        for j in range(PER_DOT):
            k = turn * PER_DOT + j
            index = map_ref[k]
            masked_banks(spread_ref[k * C : (k + 1) * C, :], index >> 8, ALL_BANKS, slot, j * VB)
            hots.append(onehot_rows(index & (LO - 1), LO))
        acc_ref[...] += lax.dot_general(
            slot[...], jnp.concatenate(hots, axis=1), NT, preferred_element_type=F32
        )


def scatter_kernel(has_start, has_faces, after_ref, start_ref, map_ref, weight_ref, pre_ref, *refs):
    if has_faces:
        own_ref, low_ref, high_ref, spread_ref, masked_ref, acc_ref = refs
    else:
        acc_ref, spread_ref, masked_ref = refs

    @pl.when(pl.program_id(0) == 0)
    def _():
        acc_ref[...] = start_ref[...] if has_start else jnp.zeros_like(acc_ref)

    scatter_step(map_ref, weight_ref, pre_ref, acc_ref, spread_ref, masked_ref)

    if has_faces:

        @pl.when(pl.program_id(0) == pl.num_programs(0) - 1)
        def _():
            own_ref[...] = acc_ref[: BANKS * C, :]
            low_ref[...] = acc_ref[BANKS * C : (BANKS + 1) * C, :].astype(BF)
            high_ref[...] = acc_ref[(BANKS + 1) * C :, :].astype(BF)


def scatter_part(part, after, start, kernel_map, weight, grad_pre):
    whole = lambda *shape: pl.BlockSpec(shape, lambda i: (0,) * len(shape))
    sums = jax.ShapeDtypeStruct((ALL_BANKS * C, LO), F32)
    scratch = [pltpu.VMEM((K * C, VB), BF), pltpu.VMEM((2, ALL_BANKS * C, PER_DOT * VB), BF)]
    at, steps, last = sum(PARTS[:part]), PARTS[part], part == len(PARTS) - 1
    if last:
        out_specs = (whole(BANKS * C, LO), whole(C, F), whole(C, F))
        out_shape = (
            jax.ShapeDtypeStruct((BANKS * C, LO), F32),
            jax.ShapeDtypeStruct((C, F), BF),
            jax.ShapeDtypeStruct((C, F), BF),
        )
        scratch.append(pltpu.VMEM(sums.shape, F32))
    else:
        out_specs, out_shape = whole(*sums.shape), sums
    return pl.pallas_call(
        functools.partial(scatter_kernel, part > 0, last),
        grid=(steps,),
        in_specs=[
            pl.BlockSpec(memory_space=pl.ANY),
            whole(*sums.shape) if part > 0 else pl.BlockSpec(memory_space=pl.ANY),
            pl.BlockSpec((K, 1, VB), lambda i: (0, 0, at + i)),
            whole(K * C, C),
            pl.BlockSpec((C, VB), lambda i: (0, at + i)),
        ],
        out_specs=out_specs,
        out_shape=out_shape,
        scratch_shapes=scratch,
        compiler_params=pltpu.CompilerParams(vmem_limit_bytes=32 << 20),
        cost_estimate=pl.CostEstimate(
            flops=2 * K * VB * steps * ALL_BANKS * C * LO, bytes_accessed=2 << 20, transcendentals=0
        ),
        name="scatter",
    )(after, start, kernel_map, weight, grad_pre)


def total_of(parts_ref):
    total = parts_ref[0].astype(F32)
    for g in range(1, GROUPS):
        total = total + parts_ref[g].astype(F32)
    return total.astype(BF)


def sum_parts_kernel(after_ref, parts_ref, out_ref):
    total = total_of(parts_ref)
    for g in range(GROUPS):
        out_ref[g] = total


def sum_parts(after, parts):
    return pl.pallas_call(
        sum_parts_kernel,
        in_specs=[pl.BlockSpec(memory_space=pl.ANY), pl.BlockSpec(memory_space=pltpu.VMEM)],
        out_shape=jax.ShapeDtypeStruct(parts.shape, BF),
        compiler_params=pltpu.CompilerParams(vmem_limit_bytes=8 << 20),
        name="sum_parts",
    )(after, parts)


def fold_kernel(grad_ref, from_low_ref, from_high_ref, rows_ref, parts_ref, out_ref, masked_ref):
    share = total_of(parts_ref)
    hots = []
    for j, part_ref in enumerate((from_low_ref, from_high_ref)):
        rows = rows_ref[j : j + 1, :]
        masked_banks(part_ref[...], rows >> 8, BANKS, masked_ref, j * F)
        hots.append(onehot_rows(rows & (LO - 1), LO))
    folded = lax.dot_general(
        masked_ref[...], jnp.concatenate(hots, axis=1), NT, preferred_element_type=F32
    )
    total = (grad_ref[...] + folded).astype(BF)
    for g in range(GROUPS):
        out_ref[g, :C, :] = total[(g // 2) * C : (g // 2 + 1) * C, (g % 2) * CAP : (g % 2 + 1) * CAP]
        out_ref[g, C:, :] = share


def fold_faces(table_grad, from_low, from_high, face_rows, parts):
    return pl.pallas_call(
        fold_kernel,
        out_shape=jax.ShapeDtypeStruct((GROUPS, C + LANES, CAP), BF),
        scratch_shapes=[pltpu.VMEM((BANKS * C, 2 * F), BF)],
        compiler_params=pltpu.CompilerParams(vmem_limit_bytes=16 << 20),
        name="fold",
    )(table_grad, from_low, from_high, face_rows, parts)


def finish_kernel(scale, back_ref, owner_ref, slot_ref, out_ref, wg_ref, flat_ref):
    table = back_ref[:, :C, :].reshape(GROUPS * C, CAP)
    for b in range(R // LO):
        cols = slice(b * LO, (b + 1) * LO)
        product = jnp.dot(table, onehot_rows(slot_ref[:, cols], CAP), preferred_element_type=F32)
        out_ref[:, cols] = select_banks(product, owner_ref[:, cols], GROUPS).astype(BF)
    for t in range(TILES + 1):
        for i in range(C // 16):
            shard, slot = tile_place(i, t)
            tile = back_ref[shard, C + slot * 16 : C + (slot + 1) * 16, :].astype(F32) * scale
            flat_ref[i * 16 : (i + 1) * 16, t * LANES : (t + 1) * LANES] = tile
    for k in range(K):
        wg_ref[k] = flat_ref[:, k * C : (k + 1) * C]


def finish(returned, owner, slot, scale):
    return pl.pallas_call(
        functools.partial(finish_kernel, scale),
        out_shape=(jax.ShapeDtypeStruct((C, R), BF), jax.ShapeDtypeStruct((K, C, C), F32)),
        scratch_shapes=[pltpu.VMEM((C, (TILES + 1) * LANES), F32)],
        compiler_params=pltpu.CompilerParams(vmem_limit_bytes=24 << 20),
        name="finish",
    )(returned, owner, slot)


def body(points, owners, kernel_maps, face_rows, weight, cotangent):
    points, owner = points[0, 0], owners.reshape(1, R)
    kernel_map, face_list, incoming = kernel_maps.reshape(K, 1, V), face_rows[0, 0], cotangent[0, 0]
    side = lax.axis_size("sy")
    up = [(i, i + 1) for i in range(side - 1)]
    down = [(i + 1, i) for i in range(side - 1)]

    outgoing, slot = place_points(points, owner)
    owned = lax.all_to_all(outgoing, "sx", 0, 0, tiled=True)
    lower, upper = take_faces(owned, face_list)
    ghost_low = lax.ppermute(upper, "sy", up)
    ghost_high = lax.ppermute(lower, "sy", down)
    weight_rows = jnp.transpose(weight, (1, 0, 2)).reshape(C, K * C)
    output, grad_pre, weight_part = forward_pass(
        owned, ghost_low, ghost_high, kernel_map, weight_rows, incoming
    )
    weight_columns = jnp.transpose(weight, (0, 2, 1)).reshape(K * C, C)
    scatter = functools.partial(scatter_part, kernel_map=kernel_map, weight=weight_columns, grad_pre=grad_pre)
    across = lambda array, axis: lax.all_to_all(array, axis, 0, 0, tiled=True)
    parts = across(weight_part, "sx")
    sums = scatter(0, grad_pre, grad_pre)
    row_sums = sum_parts(sums, parts)
    parts = across(row_sums, "sy")
    sums = scatter(1, row_sums, sums)
    table_grad, to_low, to_high = scatter(2, parts, sums)
    from_low = lax.ppermute(to_high, "sy", up)
    from_high = lax.ppermute(to_low, "sy", down)
    owned_grad = fold_faces(table_grad, from_low, from_high, face_list, parts)
    returned = across(owned_grad, "sx")
    scale = 1.0 / math.sqrt(GROUPS * side * V)
    point_grad, weight_grad = finish(returned, owner, slot, scale)
    return (output[None, None], point_grad[None, None], weight_grad)


def solution(mesh):
    split = P("sx", "sy", None, None)
    return jax.shard_map(
        body,
        mesh=mesh,
        in_specs=(split, split, split, split, P(), split),
        out_specs=(split, split, P()),
        check_vma=False,
    )
```

```python
import functools
import math

import jax
import jax.numpy as jnp
from jax import lax
from jax.experimental import pallas as pl
from jax.experimental.pallas import tpu as pltpu
from jax.sharding import PartitionSpec as P

C = 96
K = 27
R = 1024
F = 256
CAP = 128
V = 2048
GROUPS = 16
LO = 256
BANKS = V // LO
ALL_BANKS = BANKS + 2
WIDE = 512
WIDE_BANKS = ALL_BANKS * LO // WIDE
VB = 256
FORWARD_VB = 512
PER_DOT = 3
PARTS = (1, 2, 2, 2, 1)
LANES = 128
TILES = K * C // LANES
SHARD_TILES = 4
HALF = SHARD_TILES * 16

BF = jnp.bfloat16
F32 = jnp.float32
NT = (((1,), (1,)), ((), ()))


def rows16(index):
    return jnp.broadcast_to(index, (16, index.shape[-1])).astype(jnp.int16)


def onehot_rows(low, rows):
    n = low.shape[-1]
    row = lax.broadcasted_iota(jnp.int16, (rows, n), 0).reshape(rows // 16, 16, n)
    return jnp.where(row == rows16(low)[None], BF(1), BF(0)).reshape(rows, n)


def select_banks(product, bank, banks):
    n = bank.shape[-1]
    bank8 = jnp.broadcast_to(bank, (8, n))
    kept = jnp.zeros((C // 8, 8, n), F32)
    for a in range(banks):
        part = product[a * C : (a + 1) * C].reshape(C // 8, 8, n)
        kept = jnp.where((bank8 == a)[None], part, kept)
    return kept.reshape(C, n)


def masked_banks(values, bank, banks, out_ref, column):
    n = bank.shape[-1]
    bank16 = rows16(bank)
    values = values.reshape(C // 16, 16, n)
    for a in range(banks):
        spread = jnp.where((bank16 == a)[None], values, BF(0))
        out_ref[a * C : (a + 1) * C, column : column + n] = spread.reshape(C, n)


def tile_place(i, t):
    rest, slot = divmod(i * TILES + t if t < TILES else (C // 16) * TILES + i, SHARD_TILES)
    return *divmod(rest, GROUPS), slot


def place_kernel(points_ref, owner_ref, out_ref, slot_ref, masked_ref):
    owner = owner_ref[...]
    row = lax.broadcasted_iota(jnp.int32, (CAP, CAP), 0)
    col = lax.broadcasted_iota(jnp.int32, (CAP, CAP), 1)
    earlier = jnp.where(row < col, 1.0, 0.0).astype(BF)
    group = lax.broadcasted_iota(jnp.int32, (GROUPS, CAP), 0)
    total = jnp.zeros((GROUPS, 1), F32)
    for b in range(R // CAP):
        mine = jnp.where(group == owner[:, b * CAP : (b + 1) * CAP], 1.0, 0.0)
        before = jnp.dot(mine.astype(BF), earlier, preferred_element_type=F32) + total
        slot = jnp.sum(mine * before, axis=0, keepdims=True)
        slot_ref[:, b * CAP : (b + 1) * CAP] = slot.astype(jnp.int32)
        total = total + jnp.sum(mine, axis=1, keepdims=True)
    masked_banks(points_ref[...], owner, GROUPS, masked_ref, 0)
    onehot = onehot_rows(slot_ref[...], CAP)
    for g in range(GROUPS):
        out_ref[g] = lax.dot_general(
            masked_ref[g * C : (g + 1) * C, :], onehot, NT, preferred_element_type=F32
        ).astype(BF)


def place_points(points, owner):
    return pl.pallas_call(
        place_kernel,
        out_shape=(
            jax.ShapeDtypeStruct((GROUPS, C, CAP), BF),
            jax.ShapeDtypeStruct((1, R), jnp.int32),
        ),
        scratch_shapes=[pltpu.VMEM((GROUPS * C, R), BF)],
        compiler_params=pltpu.CompilerParams(vmem_limit_bytes=16 << 20),
        name="place",
    )(points, owner)


def faces_kernel(owned_ref, rows_ref, lower_ref, upper_ref):
    table = owned_ref[...].reshape(GROUPS * C, CAP)
    for j, out_ref in enumerate((lower_ref, upper_ref)):
        rows = rows_ref[j : j + 1, :]
        product = jnp.dot(table, onehot_rows(rows & (CAP - 1), CAP), preferred_element_type=F32)
        out_ref[...] = select_banks(product, rows >> 7, GROUPS).astype(BF)


def take_faces(owned, face_rows):
    return pl.pallas_call(
        faces_kernel,
        out_shape=(jax.ShapeDtypeStruct((C, F), BF),) * 2,
        compiler_params=pltpu.CompilerParams(vmem_limit_bytes=16 << 20),
        name="faces",
    )(owned, face_rows)


def forward_kernel(
    owned_ref, low_ref, high_ref, map_ref, weight_ref, cot_ref, out_ref, pre_ref, wg_ref, table_ref, picked_ref, acc_ref
):
    step = pl.program_id(0)

    @pl.when(step == 0)
    def _():
        per = WIDE // CAP
        for g in range(GROUPS):
            table_ref[(g // per) * C : (g // per + 1) * C, (g % per) * CAP : (g % per + 1) * CAP] = owned_ref[g]
        table_ref[(WIDE_BANKS - 1) * C :, :F] = low_ref[...]
        table_ref[(WIDE_BANKS - 1) * C :, F:] = high_ref[...]
        acc_ref[...] = jnp.zeros_like(acc_ref)

    table = table_ref[...]
    for k in range(K):
        index = map_ref[k]
        product = jnp.dot(table, onehot_rows(index & (WIDE - 1), WIDE), preferred_element_type=F32)
        picked_ref[k * C : (k + 1) * C, :] = select_banks(product, index >> 9, WIDE_BANKS).astype(BF)
    preact = jnp.dot(weight_ref[...], picked_ref[...], preferred_element_type=F32)
    logistic = jax.nn.sigmoid(preact)
    out_ref[...] = (preact * logistic).astype(BF)
    slope = logistic * (1.0 + preact * (1.0 - logistic))
    grad_pre = (cot_ref[...].astype(F32) * slope).astype(BF)
    pre_ref[...] = grad_pre
    acc_ref[...] += lax.dot_general(picked_ref[...], grad_pre, NT, preferred_element_type=F32)

    @pl.when(step == pl.num_programs(0) - 1)
    def _():
        for t in range(TILES + 1):
            block = acc_ref[t * LANES : min((t + 1) * LANES, K * C), :].T
            if t == TILES:
                block = jnp.concatenate([block, jnp.zeros((C, LANES - block.shape[1]), F32)], axis=1)
            block = block.astype(BF)
            for i in range(C // 16):
                half, shard, slot = tile_place(i, t)
                wg_ref[half, shard, slot * 16 : (slot + 1) * 16, :] = block[i * 16 : (i + 1) * 16, :]
        used = (TILES + 1) * (C // 16) - (2 * GROUPS - 1) * SHARD_TILES
        wg_ref[1, GROUPS - 1, used * 16 :, :] = jnp.zeros((HALF - used * 16, LANES), BF)


def forward_pass(owned, low, high, kernel_map, weight, cotangent):
    whole = lambda *shape: pl.BlockSpec(shape, lambda i: (0,) * len(shape))
    column = lambda rows: pl.BlockSpec((rows, FORWARD_VB), lambda i: (0, i))
    return pl.pallas_call(
        forward_kernel,
        grid=(V // FORWARD_VB,),
        in_specs=[
            whole(GROUPS, C, CAP),
            whole(C, F),
            whole(C, F),
            pl.BlockSpec((K, 1, FORWARD_VB), lambda i: (0, 0, i)),
            whole(C, K * C),
            column(C),
        ],
        out_specs=(column(C), column(C), whole(2, GROUPS, HALF, LANES)),
        out_shape=(
            jax.ShapeDtypeStruct((C, V), BF),
            jax.ShapeDtypeStruct((C, V), BF),
            jax.ShapeDtypeStruct((2, GROUPS, HALF, LANES), BF),
        ),
        scratch_shapes=[
            pltpu.VMEM((WIDE_BANKS * C, WIDE), BF),
            pltpu.VMEM((K * C, FORWARD_VB), BF),
            pltpu.VMEM((K * C, C), F32),
        ],
        compiler_params=pltpu.CompilerParams(vmem_limit_bytes=24 << 20),
        cost_estimate=pl.CostEstimate(
            flops=2 * K * V * ALL_BANKS * C * LO, bytes_accessed=4 << 20, transcendentals=C * V
        ),
        name="gather_forward",
    )(owned, low, high, kernel_map, weight, cotangent)


def scatter_step(map_ref, weight_ref, pre_ref, acc_ref, spread_ref, masked_ref):
    spread_ref[...] = jnp.dot(weight_ref[...], pre_ref[...], preferred_element_type=F32).astype(BF)
    for turn in range(K // PER_DOT):
        hots = []
        slot = masked_ref.at[turn % 2]
        for j in range(PER_DOT):
            k = turn * PER_DOT + j
            index = map_ref[k]
            masked_banks(spread_ref[k * C : (k + 1) * C, :], index >> 8, ALL_BANKS, slot, j * VB)
            hots.append(onehot_rows(index & (LO - 1), LO))
        acc_ref[...] += lax.dot_general(
            slot[...], jnp.concatenate(hots, axis=1), NT, preferred_element_type=F32
        )


def scatter_kernel(has_start, has_faces, after_ref, start_ref, map_ref, weight_ref, pre_ref, *refs):
    if has_faces:
        own_ref, low_ref, high_ref, spread_ref, masked_ref, acc_ref = refs
    else:
        acc_ref, spread_ref, masked_ref = refs

    @pl.when(pl.program_id(0) == 0)
    def _():
        acc_ref[...] = start_ref[...] if has_start else jnp.zeros_like(acc_ref)

    scatter_step(map_ref, weight_ref, pre_ref, acc_ref, spread_ref, masked_ref)

    if has_faces:

        @pl.when(pl.program_id(0) == pl.num_programs(0) - 1)
        def _():
            own_ref[...] = acc_ref[: BANKS * C, :]
            low_ref[...] = acc_ref[BANKS * C : (BANKS + 1) * C, :].astype(BF)
            high_ref[...] = acc_ref[(BANKS + 1) * C :, :].astype(BF)


def scatter_part(part, after, start, kernel_map, weight, grad_pre):
    whole = lambda *shape: pl.BlockSpec(shape, lambda i: (0,) * len(shape))
    sums = jax.ShapeDtypeStruct((ALL_BANKS * C, LO), F32)
    scratch = [pltpu.VMEM((K * C, VB), BF), pltpu.VMEM((2, ALL_BANKS * C, PER_DOT * VB), BF)]
    at, steps, last = sum(PARTS[:part]), PARTS[part], part == len(PARTS) - 1
    if last:
        out_specs = (whole(BANKS * C, LO), whole(C, F), whole(C, F))
        out_shape = (
            jax.ShapeDtypeStruct((BANKS * C, LO), F32),
            jax.ShapeDtypeStruct((C, F), BF),
            jax.ShapeDtypeStruct((C, F), BF),
        )
        scratch.append(pltpu.VMEM(sums.shape, F32))
    else:
        out_specs, out_shape = whole(*sums.shape), sums
    return pl.pallas_call(
        functools.partial(scatter_kernel, part > 0, last),
        grid=(steps,),
        in_specs=[
            pl.BlockSpec(memory_space=pl.ANY),
            whole(*sums.shape) if part > 0 else pl.BlockSpec(memory_space=pl.ANY),
            pl.BlockSpec((K, 1, VB), lambda i: (0, 0, at + i)),
            whole(K * C, C),
            pl.BlockSpec((C, VB), lambda i: (0, at + i)),
        ],
        out_specs=out_specs,
        out_shape=out_shape,
        scratch_shapes=scratch,
        compiler_params=pltpu.CompilerParams(vmem_limit_bytes=18 << 20),
        cost_estimate=pl.CostEstimate(
            flops=2 * K * VB * steps * ALL_BANKS * C * LO, bytes_accessed=2 << 20, transcendentals=0
        ),
        name="scatter",
    )(after, start, kernel_map, weight, grad_pre)


def sum_parts_kernel(after_ref, parts_ref, out_ref):
    total = parts_ref[0].astype(F32)
    for g in range(1, parts_ref.shape[0]):
        total = total + parts_ref[g].astype(F32)
    total = total.astype(BF)
    if len(out_ref.shape) == len(total.shape):
        out_ref[...] = total
    else:
        for g in range(out_ref.shape[0]):
            out_ref[g] = total


def sum_parts(after, parts, copies=None):
    shape = parts.shape[1:] if copies is None else (copies, *parts.shape[1:])
    return pl.pallas_call(
        sum_parts_kernel,
        in_specs=[pl.BlockSpec(memory_space=pl.ANY), pl.BlockSpec(memory_space=pltpu.VMEM)],
        out_shape=jax.ShapeDtypeStruct(shape, BF),
        compiler_params=pltpu.CompilerParams(vmem_limit_bytes=8 << 20),
        name="sum_parts",
    )(after, parts)


def fold_kernel(grad_ref, from_low_ref, from_high_ref, rows_ref, parts_ref, out_ref, both_ref, masked_ref):
    for half in range(2):
        both_ref[half] = parts_ref[...]
    hots = []
    for j, part_ref in enumerate((from_low_ref, from_high_ref)):
        rows = rows_ref[j : j + 1, :]
        masked_banks(part_ref[...], rows >> 8, BANKS, masked_ref, j * F)
        hots.append(onehot_rows(rows & (LO - 1), LO))
    folded = lax.dot_general(
        masked_ref[...], jnp.concatenate(hots, axis=1), NT, preferred_element_type=F32
    )
    total = (grad_ref[...] + folded).astype(BF)
    for g in range(GROUPS):
        out_ref[g] = total[(g // 2) * C : (g // 2 + 1) * C, (g % 2) * CAP : (g % 2 + 1) * CAP]


def fold_faces(table_grad, from_low, from_high, face_rows, parts):
    return pl.pallas_call(
        fold_kernel,
        out_shape=(
            jax.ShapeDtypeStruct((GROUPS, C, CAP), BF),
            jax.ShapeDtypeStruct((2, *parts.shape), BF),
        ),
        scratch_shapes=[pltpu.VMEM((BANKS * C, 2 * F), BF)],
        compiler_params=pltpu.CompilerParams(vmem_limit_bytes=16 << 20),
        name="fold",
    )(table_grad, from_low, from_high, face_rows, parts)


def finish_kernel(scale, back_ref, owner_ref, slot_ref, parts_ref, out_ref, wg_ref, flat_ref):
    table = back_ref[...].reshape(GROUPS * C, CAP)
    for b in range(R // LO):
        cols = slice(b * LO, (b + 1) * LO)
        product = jnp.dot(table, onehot_rows(slot_ref[:, cols], CAP), preferred_element_type=F32)
        out_ref[:, cols] = select_banks(product, owner_ref[:, cols], GROUPS).astype(BF)
    for t in range(TILES + 1):
        for i in range(C // 16):
            half, shard, slot = tile_place(i, t)
            tile = parts_ref[half, shard, slot * 16 : (slot + 1) * 16, :].astype(F32) * scale
            flat_ref[i * 16 : (i + 1) * 16, t * LANES : (t + 1) * LANES] = tile
    for k in range(K):
        wg_ref[k] = flat_ref[:, k * C : (k + 1) * C]


def finish(returned, owner, slot, parts, scale):
    return pl.pallas_call(
        functools.partial(finish_kernel, scale),
        out_shape=(jax.ShapeDtypeStruct((C, R), BF), jax.ShapeDtypeStruct((K, C, C), F32)),
        scratch_shapes=[pltpu.VMEM((C, (TILES + 1) * LANES), F32)],
        compiler_params=pltpu.CompilerParams(vmem_limit_bytes=24 << 20),
        name="finish",
    )(returned, owner, slot, parts)


def body(points, owners, kernel_maps, face_rows, weight, cotangent):
    points, owner = points[0, 0], owners.reshape(1, R)
    kernel_map, face_list, incoming = kernel_maps.reshape(K, 1, V), face_rows[0, 0], cotangent[0, 0]
    side = lax.axis_size("sy")
    up = [(i, i + 1) for i in range(side - 1)]
    down = [(i + 1, i) for i in range(side - 1)]

    outgoing, slot = place_points(points, owner)
    owned = lax.all_to_all(outgoing, "sx", 0, 0, tiled=True)
    lower, upper = take_faces(owned, face_list)
    ghost_low = lax.ppermute(upper, "sy", up)
    ghost_high = lax.ppermute(lower, "sy", down)
    weight_rows = jnp.transpose(weight, (1, 0, 2)).reshape(C, K * C)
    output, grad_pre, weight_part = forward_pass(
        owned, ghost_low, ghost_high, kernel_map, weight_rows, incoming
    )
    weight_columns = jnp.transpose(weight, (0, 2, 1)).reshape(K * C, C)
    scatter = functools.partial(scatter_part, kernel_map=kernel_map, weight=weight_columns, grad_pre=grad_pre)

    def across(array, axis, groups=None):
        return lax.all_to_all(array, axis, 0, 0, axis_index_groups=groups, tiled=True)

    pairs = [[2 * i, 2 * i + 1] for i in range(side // 2)]
    chips = [list(range(core, side, 2)) for core in range(2)]
    parts = across(weight_part, "sy", pairs)
    sums = scatter(0, grad_pre, grad_pre)
    pair_sum = sum_parts(sums, parts)
    parts = across(pair_sum, "sx")
    sums = scatter(1, pair_sum, sums)
    row_sums = sum_parts(sums, parts, side // 2)
    parts = across(row_sums, "sy", chips)
    sums = scatter(2, row_sums, sums)
    all_sums = sum_parts(sums, parts, GROUPS)
    parts = across(all_sums, "sx")
    sums = scatter(3, all_sums, sums)
    table_grad, to_low, to_high = scatter(4, parts, sums)
    from_low = lax.ppermute(to_high, "sy", up)
    from_high = lax.ppermute(to_low, "sy", down)
    owned_grad, both = fold_faces(table_grad, from_low, from_high, face_list, parts)
    parts = across(both, "sy", pairs)
    returned = across(owned_grad, "sx")
    scale = 1.0 / math.sqrt(GROUPS * side * V)
    point_grad, weight_grad = finish(returned, owner, slot, parts, scale)
    return (output[None, None], point_grad[None, None], weight_grad)


def solution(mesh):
    split = P("sx", "sy", None, None)
    return jax.shard_map(
        body,
        mesh=mesh,
        in_specs=(split, split, split, split, P(), split),
        out_specs=(split, split, P()),
        check_vma=False,
    )
```

```python
import functools
import math

import jax
import jax.numpy as jnp
from jax import lax
from jax.experimental import pallas as pl
from jax.experimental.pallas import tpu as pltpu
from jax.sharding import PartitionSpec as P

C = 96
K = 27
R = 1024
F = 256
CAP = 128
V = 2048
GROUPS = 16
LO = 256
BANKS = V // LO
ALL_BANKS = BANKS + 2
WIDE = 512
WIDE_BANKS = ALL_BANKS * LO // WIDE
VB = 256
FORWARD_VB = 512
MAIN = 80
PER_DOT = 3
PARTS = (3, 3, 2)
LANES = 128
TILES = K * C // LANES
SHARD_TILES = 8

BF = jnp.bfloat16
F32 = jnp.float32
NT = (((1,), (1,)), ((), ()))


def rows16(index):
    return jnp.broadcast_to(index, (16, index.shape[-1])).astype(jnp.int16)


def onehot_rows(low, rows):
    n = low.shape[-1]
    row = lax.broadcasted_iota(jnp.int16, (rows, n), 0).reshape(rows // 16, 16, n)
    return jnp.where(row == rows16(low)[None], BF(1), BF(0)).reshape(rows, n)


def select_banks(product, bank, banks, channels=C):
    n = bank.shape[-1]
    bank8 = jnp.broadcast_to(bank, (8, n))
    kept = jnp.zeros((channels // 8, 8, n), F32)
    for a in range(banks):
        part = product[a * channels : (a + 1) * channels].reshape(channels // 8, 8, n)
        kept = jnp.where((bank8 == a)[None], part, kept)
    return kept.reshape(channels, n)


LANE_GATHER = lax.GatherDimensionNumbers(
    offset_dims=(),
    collapsed_slice_dims=(1,),
    start_index_map=(1,),
    operand_batching_dims=(0,),
    start_indices_batching_dims=(0,),
)


def gather_lanes(tiles_ref, index):
    lane, tile = rows16(index & (CAP - 1)), rows16(index >> 7)
    kept = jnp.zeros((16, CAP), BF)
    for t in range(tiles_ref.shape[0]):
        read = lax.gather(
            tiles_ref[t], lane[..., None], LANE_GATHER, (1, 1), mode=lax.GatherScatterMode.PROMISE_IN_BOUNDS
        )
        kept = jnp.where(tile == t, read, kept)
    return kept


def masked_banks(values, bank, banks, out_ref, column):
    n = bank.shape[-1]
    bank16 = rows16(bank)
    values = values.reshape(C // 16, 16, n)
    for a in range(banks):
        spread = jnp.where((bank16 == a)[None], values, BF(0))
        out_ref[a * C : (a + 1) * C, column : column + n] = spread.reshape(C, n)


def tile_place(i, t):
    return divmod(i * TILES + t if t < TILES else (C // 16) * TILES + i, SHARD_TILES)


def place_kernel(points_ref, owner_ref, out_ref, slot_ref, masked_ref):
    owner = owner_ref[...]
    row = lax.broadcasted_iota(jnp.int32, (CAP, CAP), 0)
    col = lax.broadcasted_iota(jnp.int32, (CAP, CAP), 1)
    earlier = jnp.where(row < col, 1.0, 0.0).astype(BF)
    group = lax.broadcasted_iota(jnp.int32, (GROUPS, CAP), 0)
    total = jnp.zeros((GROUPS, 1), F32)
    for b in range(R // CAP):
        mine = jnp.where(group == owner[:, b * CAP : (b + 1) * CAP], 1.0, 0.0)
        before = jnp.dot(mine.astype(BF), earlier, preferred_element_type=F32) + total
        slot = jnp.sum(mine * before, axis=0, keepdims=True)
        slot_ref[:, b * CAP : (b + 1) * CAP] = slot.astype(jnp.int32)
        total = total + jnp.sum(mine, axis=1, keepdims=True)
    masked_banks(points_ref[...], owner, GROUPS, masked_ref, 0)
    onehot = onehot_rows(slot_ref[...], CAP)
    for g in range(GROUPS):
        out_ref[g] = lax.dot_general(
            masked_ref[g * C : (g + 1) * C, :], onehot, NT, preferred_element_type=F32
        ).astype(BF)


def place_points(points, owner):
    return pl.pallas_call(
        place_kernel,
        out_shape=(
            jax.ShapeDtypeStruct((GROUPS, C, CAP), BF),
            jax.ShapeDtypeStruct((1, R), jnp.int32),
        ),
        scratch_shapes=[pltpu.VMEM((GROUPS * C, R), BF)],
        compiler_params=pltpu.CompilerParams(vmem_limit_bytes=16 << 20),
        name="place",
    )(points, owner)


def faces_kernel(owned_ref, rows_ref, lower_ref, upper_ref):
    table = owned_ref[...].reshape(GROUPS * C, CAP)
    for j, out_ref in enumerate((lower_ref, upper_ref)):
        rows = rows_ref[j : j + 1, :]
        product = jnp.dot(table, onehot_rows(rows & (CAP - 1), CAP), preferred_element_type=F32)
        out_ref[...] = select_banks(product, rows >> 7, GROUPS).astype(BF)


def take_faces(owned, face_rows):
    return pl.pallas_call(
        faces_kernel,
        out_shape=(jax.ShapeDtypeStruct((C, F), BF),) * 2,
        compiler_params=pltpu.CompilerParams(vmem_limit_bytes=16 << 20),
        name="faces",
    )(owned, face_rows)


def forward_kernel(
    owned_ref, low_ref, high_ref, map_ref, weight_ref, cot_ref, out_ref, pre_ref, wg_ref, table_ref, tail_ref, picked_ref, acc_ref
):
    step = pl.program_id(0)

    @pl.when(step == 0)
    def _():
        per = WIDE // CAP
        for g in range(GROUPS):
            rows = slice((g // per) * MAIN, (g // per + 1) * MAIN)
            table_ref[rows, (g % per) * CAP : (g % per + 1) * CAP] = owned_ref[g, :MAIN, :]
            tail_ref[g] = owned_ref[g, MAIN:, :]
        table_ref[(WIDE_BANKS - 1) * MAIN :, :F] = low_ref[:MAIN, :]
        table_ref[(WIDE_BANKS - 1) * MAIN :, F:] = high_ref[:MAIN, :]
        for j, ghost_ref in enumerate((low_ref, high_ref)):
            for i in range(F // CAP):
                tail_ref[GROUPS + j * (F // CAP) + i] = ghost_ref[MAIN:, i * CAP : (i + 1) * CAP]
        acc_ref[...] = jnp.zeros_like(acc_ref)

    table = table_ref[...]
    for k in range(K):
        index = map_ref[k]
        product = jnp.dot(table, onehot_rows(index & (WIDE - 1), WIDE), preferred_element_type=F32)
        main = select_banks(product, index >> 9, WIDE_BANKS, MAIN)
        picked_ref[k * C : k * C + MAIN, :] = main.astype(BF)
        for i in range(FORWARD_VB // CAP):
            cols = slice(i * CAP, (i + 1) * CAP)
            picked_ref[k * C + MAIN : (k + 1) * C, cols] = gather_lanes(tail_ref, index[:, cols])
    preact = jnp.dot(weight_ref[...], picked_ref[...], preferred_element_type=F32)
    logistic = jax.nn.sigmoid(preact)
    out_ref[...] = (preact * logistic).astype(BF)
    slope = logistic * (1.0 + preact * (1.0 - logistic))
    grad_pre = (cot_ref[...].astype(F32) * slope).astype(BF)
    pre_ref[...] = grad_pre
    acc_ref[...] += lax.dot_general(picked_ref[...], grad_pre, NT, preferred_element_type=F32)

    @pl.when(step == pl.num_programs(0) - 1)
    def _():
        for t in range(TILES + 1):
            block = acc_ref[t * LANES : min((t + 1) * LANES, K * C), :].T
            if t == TILES:
                block = jnp.concatenate([block, jnp.zeros((C, LANES - block.shape[1]), F32)], axis=1)
            block = block.astype(BF)
            for i in range(C // 16):
                shard, slot = tile_place(i, t)
                wg_ref[shard, slot * 16 : (slot + 1) * 16, :] = block[i * 16 : (i + 1) * 16, :]
        used = (TILES + 1) * (C // 16) - (GROUPS - 1) * SHARD_TILES
        wg_ref[GROUPS - 1, used * 16 :, :] = jnp.zeros((LANES - used * 16, LANES), BF)


def forward_pass(owned, low, high, kernel_map, weight, cotangent):
    whole = lambda *shape: pl.BlockSpec(shape, lambda i: (0,) * len(shape))
    column = lambda rows: pl.BlockSpec((rows, FORWARD_VB), lambda i: (0, i))
    return pl.pallas_call(
        forward_kernel,
        grid=(V // FORWARD_VB,),
        in_specs=[
            whole(GROUPS, C, CAP),
            whole(C, F),
            whole(C, F),
            pl.BlockSpec((K, 1, FORWARD_VB), lambda i: (0, 0, i)),
            whole(C, K * C),
            column(C),
        ],
        out_specs=(column(C), column(C), whole(GROUPS, LANES, LANES)),
        out_shape=(
            jax.ShapeDtypeStruct((C, V), BF),
            jax.ShapeDtypeStruct((C, V), BF),
            jax.ShapeDtypeStruct((GROUPS, LANES, LANES), BF),
        ),
        scratch_shapes=[
            pltpu.VMEM((WIDE_BANKS * MAIN, WIDE), BF),
            pltpu.VMEM((V // CAP + 2 * F // CAP, C - MAIN, CAP), BF),
            pltpu.VMEM((K * C, FORWARD_VB), BF),
            pltpu.VMEM((K * C, C), F32),
        ],
        compiler_params=pltpu.CompilerParams(vmem_limit_bytes=32 << 20),
        cost_estimate=pl.CostEstimate(
            flops=2 * K * V * ALL_BANKS * C * LO, bytes_accessed=4 << 20, transcendentals=C * V
        ),
        name="gather_forward",
    )(owned, low, high, kernel_map, weight, cotangent)


def bank_rows(values, bank):
    n = bank.shape[-1]
    bank16 = rows16(bank)
    values = values.reshape(C // 16, 16, n)
    banks = [jnp.where((bank16 == a)[None], values, BF(0)).reshape(C, n) for a in range(ALL_BANKS)]
    return jnp.concatenate(banks, axis=0)


def scatter_step(map_ref, weight_ref, pre_ref, acc_ref, spread_ref):
    spread_ref[...] = jnp.dot(weight_ref[...], pre_ref[...], preferred_element_type=F32).astype(BF)
    for first in range(0, K, PER_DOT):
        spreads, hots = [], []
        for k in range(first, first + PER_DOT):
            index = map_ref[k]
            spreads.append(bank_rows(spread_ref[k * C : (k + 1) * C, :], index >> 8))
            hots.append(onehot_rows(index & (LO - 1), LO))
        acc_ref[...] += lax.dot_general(
            jnp.concatenate(spreads, axis=1), jnp.concatenate(hots, axis=1), NT, preferred_element_type=F32
        )


def scatter_kernel(has_start, has_faces, after_ref, start_ref, map_ref, weight_ref, pre_ref, *refs):
    if has_faces:
        own_ref, low_ref, high_ref, spread_ref, acc_ref = refs
    else:
        acc_ref, spread_ref = refs

    @pl.when(pl.program_id(0) == 0)
    def _():
        acc_ref[...] = start_ref[...] if has_start else jnp.zeros_like(acc_ref)

    scatter_step(map_ref, weight_ref, pre_ref, acc_ref, spread_ref)

    if has_faces:

        @pl.when(pl.program_id(0) == pl.num_programs(0) - 1)
        def _():
            own_ref[...] = acc_ref[: BANKS * C, :]
            low_ref[...] = acc_ref[BANKS * C : (BANKS + 1) * C, :].astype(BF)
            high_ref[...] = acc_ref[(BANKS + 1) * C :, :].astype(BF)


def scatter_part(part, after, start, kernel_map, weight, grad_pre):
    whole = lambda *shape: pl.BlockSpec(shape, lambda i: (0,) * len(shape))
    sums = jax.ShapeDtypeStruct((ALL_BANKS * C, LO), F32)
    scratch = [pltpu.VMEM((K * C, VB), BF)]
    at, steps, last = sum(PARTS[:part]), PARTS[part], part == len(PARTS) - 1
    if last:
        out_specs = (whole(BANKS * C, LO), whole(C, F), whole(C, F))
        out_shape = (
            jax.ShapeDtypeStruct((BANKS * C, LO), F32),
            jax.ShapeDtypeStruct((C, F), BF),
            jax.ShapeDtypeStruct((C, F), BF),
        )
        scratch.append(pltpu.VMEM(sums.shape, F32))
    else:
        out_specs, out_shape = whole(*sums.shape), sums
    return pl.pallas_call(
        functools.partial(scatter_kernel, part > 0, last),
        grid=(steps,),
        in_specs=[
            pl.BlockSpec(memory_space=pl.ANY),
            whole(*sums.shape) if part > 0 else pl.BlockSpec(memory_space=pl.ANY),
            pl.BlockSpec((K, 1, VB), lambda i: (0, 0, at + i)),
            whole(K * C, C),
            pl.BlockSpec((C, VB), lambda i: (0, at + i)),
        ],
        out_specs=out_specs,
        out_shape=out_shape,
        scratch_shapes=scratch,
        compiler_params=pltpu.CompilerParams(vmem_limit_bytes=24 << 20),
        cost_estimate=pl.CostEstimate(
            flops=2 * K * VB * steps * ALL_BANKS * C * LO, bytes_accessed=2 << 20, transcendentals=0
        ),
        name="scatter",
    )(after, start, kernel_map, weight, grad_pre)


def total_of(parts_ref):
    total = parts_ref[0].astype(F32)
    for g in range(1, GROUPS):
        total = total + parts_ref[g].astype(F32)
    return total.astype(BF)


def sum_parts_kernel(after_ref, parts_ref, out_ref):
    total = total_of(parts_ref)
    for g in range(GROUPS):
        out_ref[g] = total


def sum_parts(after, parts):
    return pl.pallas_call(
        sum_parts_kernel,
        in_specs=[pl.BlockSpec(memory_space=pl.ANY), pl.BlockSpec(memory_space=pltpu.VMEM)],
        out_shape=jax.ShapeDtypeStruct(parts.shape, BF),
        compiler_params=pltpu.CompilerParams(vmem_limit_bytes=8 << 20),
        name="sum_parts",
    )(after, parts)


def fold_kernel(grad_ref, from_low_ref, from_high_ref, rows_ref, parts_ref, out_ref, masked_ref):
    share = total_of(parts_ref)
    hots = []
    for j, part_ref in enumerate((from_low_ref, from_high_ref)):
        rows = rows_ref[j : j + 1, :]
        masked_banks(part_ref[...], rows >> 8, BANKS, masked_ref, j * F)
        hots.append(onehot_rows(rows & (LO - 1), LO))
    folded = lax.dot_general(
        masked_ref[...], jnp.concatenate(hots, axis=1), NT, preferred_element_type=F32
    )
    total = (grad_ref[...] + folded).astype(BF)
    for g in range(GROUPS):
        out_ref[g, :C, :] = total[(g // 2) * C : (g // 2 + 1) * C, (g % 2) * CAP : (g % 2 + 1) * CAP]
        out_ref[g, C:, :] = share


def fold_faces(table_grad, from_low, from_high, face_rows, parts):
    return pl.pallas_call(
        fold_kernel,
        out_shape=jax.ShapeDtypeStruct((GROUPS, C + LANES, CAP), BF),
        scratch_shapes=[pltpu.VMEM((BANKS * C, 2 * F), BF)],
        compiler_params=pltpu.CompilerParams(vmem_limit_bytes=16 << 20),
        name="fold",
    )(table_grad, from_low, from_high, face_rows, parts)


def finish_kernel(scale, back_ref, owner_ref, slot_ref, out_ref, wg_ref, flat_ref):
    table = back_ref[:, :C, :].reshape(GROUPS * C, CAP)
    for b in range(R // LO):
        cols = slice(b * LO, (b + 1) * LO)
        product = jnp.dot(table, onehot_rows(slot_ref[:, cols], CAP), preferred_element_type=F32)
        out_ref[:, cols] = select_banks(product, owner_ref[:, cols], GROUPS).astype(BF)
    for t in range(TILES + 1):
        for i in range(C // 16):
            shard, slot = tile_place(i, t)
            tile = back_ref[shard, C + slot * 16 : C + (slot + 1) * 16, :].astype(F32) * scale
            flat_ref[i * 16 : (i + 1) * 16, t * LANES : (t + 1) * LANES] = tile
    for k in range(K):
        wg_ref[k] = flat_ref[:, k * C : (k + 1) * C]


def finish(returned, owner, slot, scale):
    return pl.pallas_call(
        functools.partial(finish_kernel, scale),
        out_shape=(jax.ShapeDtypeStruct((C, R), BF), jax.ShapeDtypeStruct((K, C, C), F32)),
        scratch_shapes=[pltpu.VMEM((C, (TILES + 1) * LANES), F32)],
        compiler_params=pltpu.CompilerParams(vmem_limit_bytes=24 << 20),
        name="finish",
    )(returned, owner, slot)


def body(points, owners, kernel_maps, face_rows, weight, cotangent):
    points, owner = points[0, 0], owners.reshape(1, R)
    kernel_map, face_list, incoming = kernel_maps.reshape(K, 1, V), face_rows[0, 0], cotangent[0, 0]
    side = lax.axis_size("sy")
    up = [(i, i + 1) for i in range(side - 1)]
    down = [(i + 1, i) for i in range(side - 1)]

    outgoing, slot = place_points(points, owner)
    owned = lax.all_to_all(outgoing, "sx", 0, 0, tiled=True)
    lower, upper = take_faces(owned, face_list)
    ghost_low = lax.ppermute(upper, "sy", up)
    ghost_high = lax.ppermute(lower, "sy", down)
    weight_rows = jnp.transpose(weight, (1, 0, 2)).reshape(C, K * C)
    output, grad_pre, weight_part = forward_pass(
        owned, ghost_low, ghost_high, kernel_map, weight_rows, incoming
    )
    weight_columns = jnp.transpose(weight, (0, 2, 1)).reshape(K * C, C)
    scatter = functools.partial(scatter_part, kernel_map=kernel_map, weight=weight_columns, grad_pre=grad_pre)
    across = lambda array, axis: lax.all_to_all(array, axis, 0, 0, tiled=True)
    parts = across(weight_part, "sx")
    sums = scatter(0, grad_pre, grad_pre)
    row_sums = sum_parts(sums, parts)
    parts = across(row_sums, "sy")
    sums = scatter(1, row_sums, sums)
    table_grad, to_low, to_high = scatter(2, parts, sums)
    from_low = lax.ppermute(to_high, "sy", up)
    from_high = lax.ppermute(to_low, "sy", down)
    owned_grad = fold_faces(table_grad, from_low, from_high, face_list, parts)
    returned = across(owned_grad, "sx")
    scale = 1.0 / math.sqrt(GROUPS * side * V)
    point_grad, weight_grad = finish(returned, owner, slot, scale)
    return (output[None, None], point_grad[None, None], weight_grad)


def solution(mesh):
    split = P("sx", "sy", None, None)
    return jax.shard_map(
        body,
        mesh=mesh,
        in_specs=(split, split, split, split, P(), split),
        out_specs=(split, split, P()),
        check_vma=False,
    )
```

```python
import functools
import math

import jax
import jax.numpy as jnp
from jax import lax
from jax.experimental import pallas as pl
from jax.experimental.pallas import tpu as pltpu
from jax.sharding import PartitionSpec as P

C = 96
K = 27
R = 1024
F = 256
CAP = 128
V = 2048
GROUPS = 16
LO = 256
BANKS = V // LO
ALL_BANKS = BANKS + 2
WIDE = 256
WIDE_BANKS = ALL_BANKS * LO // WIDE
VB = 256
FORWARD_VB = 512
MAIN = 48
PER_DOT = 3
PARTS = (3, 3, 2)
LANES = 128
TILES = K * C // LANES
SHARD_TILES = 8

BF = jnp.bfloat16
F32 = jnp.float32
NT = (((1,), (1,)), ((), ()))


def rows16(index):
    return jnp.broadcast_to(index, (16, index.shape[-1])).astype(jnp.int16)


def onehot_rows(low, rows):
    n = low.shape[-1]
    row = lax.broadcasted_iota(jnp.int16, (rows, n), 0).reshape(rows // 16, 16, n)
    return jnp.where(row == rows16(low)[None], BF(1), BF(0)).reshape(rows, n)


def select_banks(product, bank, banks, channels=C):
    n = bank.shape[-1]
    bank8 = jnp.broadcast_to(bank, (8, n))
    kept = jnp.zeros((channels // 8, 8, n), F32)
    for a in range(banks):
        part = product[a * channels : (a + 1) * channels].reshape(channels // 8, 8, n)
        kept = jnp.where((bank8 == a)[None], part, kept)
    return kept.reshape(channels, n)


LANE_GATHER = lax.GatherDimensionNumbers(
    offset_dims=(),
    collapsed_slice_dims=(1,),
    start_index_map=(1,),
    operand_batching_dims=(0,),
    start_indices_batching_dims=(0,),
)


def gather_lanes(tiles_ref, index):
    tiles, rows, _ = tiles_ref.shape
    lane, tile = rows16(index & (CAP - 1)), rows16(index >> 7)
    kept = [jnp.zeros((16, CAP), BF) for _ in range(rows // 16)]
    for t in range(tiles):
        mine = tile == t
        for h in range(rows // 16):
            read = lax.gather(
                tiles_ref[t, h * 16 : (h + 1) * 16, :],
                lane[..., None],
                LANE_GATHER,
                (1, 1),
                mode=lax.GatherScatterMode.PROMISE_IN_BOUNDS,
            )
            kept[h] = jnp.where(mine, read, kept[h])
    return jnp.concatenate(kept, axis=0)


def masked_banks(values, bank, banks, out_ref, column):
    n = bank.shape[-1]
    bank16 = rows16(bank)
    values = values.reshape(C // 16, 16, n)
    for a in range(banks):
        spread = jnp.where((bank16 == a)[None], values, BF(0))
        out_ref[a * C : (a + 1) * C, column : column + n] = spread.reshape(C, n)


def tile_place(i, t):
    return divmod(i * TILES + t if t < TILES else (C // 16) * TILES + i, SHARD_TILES)


def place_kernel(points_ref, owner_ref, out_ref, slot_ref, masked_ref):
    owner = owner_ref[...]
    row = lax.broadcasted_iota(jnp.int32, (CAP, CAP), 0)
    col = lax.broadcasted_iota(jnp.int32, (CAP, CAP), 1)
    earlier = jnp.where(row < col, 1.0, 0.0).astype(BF)
    group = lax.broadcasted_iota(jnp.int32, (GROUPS, CAP), 0)
    total = jnp.zeros((GROUPS, 1), F32)
    for b in range(R // CAP):
        mine = jnp.where(group == owner[:, b * CAP : (b + 1) * CAP], 1.0, 0.0)
        before = jnp.dot(mine.astype(BF), earlier, preferred_element_type=F32) + total
        slot = jnp.sum(mine * before, axis=0, keepdims=True)
        slot_ref[:, b * CAP : (b + 1) * CAP] = slot.astype(jnp.int32)
        total = total + jnp.sum(mine, axis=1, keepdims=True)
    masked_banks(points_ref[...], owner, GROUPS, masked_ref, 0)
    onehot = onehot_rows(slot_ref[...], CAP)
    for g in range(GROUPS):
        out_ref[g] = lax.dot_general(
            masked_ref[g * C : (g + 1) * C, :], onehot, NT, preferred_element_type=F32
        ).astype(BF)


def place_points(points, owner):
    return pl.pallas_call(
        place_kernel,
        out_shape=(
            jax.ShapeDtypeStruct((GROUPS, C, CAP), BF),
            jax.ShapeDtypeStruct((1, R), jnp.int32),
        ),
        scratch_shapes=[pltpu.VMEM((GROUPS * C, R), BF)],
        compiler_params=pltpu.CompilerParams(vmem_limit_bytes=16 << 20),
        name="place",
    )(points, owner)


def faces_kernel(owned_ref, rows_ref, lower_ref, upper_ref):
    table = owned_ref[...].reshape(GROUPS * C, CAP)
    for j, out_ref in enumerate((lower_ref, upper_ref)):
        rows = rows_ref[j : j + 1, :]
        product = jnp.dot(table, onehot_rows(rows & (CAP - 1), CAP), preferred_element_type=F32)
        out_ref[...] = select_banks(product, rows >> 7, GROUPS).astype(BF)


def take_faces(owned, face_rows):
    return pl.pallas_call(
        faces_kernel,
        out_shape=(jax.ShapeDtypeStruct((C, F), BF),) * 2,
        compiler_params=pltpu.CompilerParams(vmem_limit_bytes=16 << 20),
        name="faces",
    )(owned, face_rows)


def forward_kernel(
    owned_ref, low_ref, high_ref, map_ref, weight_ref, cot_ref, out_ref, *refs
):
    pre_refs, (wg_ref, table_ref, tail_ref, picked_ref, acc_ref) = refs[: len(PARTS)], refs[len(PARTS) :]
    step = pl.program_id(0)

    @pl.when(step == 0)
    def _():
        per = WIDE // CAP
        for g in range(GROUPS):
            rows = slice((g // per) * MAIN, (g // per + 1) * MAIN)
            table_ref[rows, (g % per) * CAP : (g % per + 1) * CAP] = owned_ref[g, :MAIN, :]
            tail_ref[g] = owned_ref[g, MAIN:, :]
        for j, ghost_ref in enumerate((low_ref, high_ref)):
            bank, at = divmod(V + j * F, WIDE)
            table_ref[bank * MAIN : (bank + 1) * MAIN, at : at + F] = ghost_ref[:MAIN, :]
            for i in range(F // CAP):
                tail_ref[GROUPS + j * (F // CAP) + i] = ghost_ref[MAIN:, i * CAP : (i + 1) * CAP]
        acc_ref[...] = jnp.zeros_like(acc_ref)

    table = table_ref[...]
    for k in range(K):
        index = map_ref[k]
        product = jnp.dot(table, onehot_rows(index & (WIDE - 1), WIDE), preferred_element_type=F32)
        main = select_banks(product, index >> (WIDE.bit_length() - 1), WIDE_BANKS, MAIN)
        picked_ref[k * C : k * C + MAIN, :] = main.astype(BF)
        for i in range(FORWARD_VB // CAP):
            cols = slice(i * CAP, (i + 1) * CAP)
            picked_ref[k * C + MAIN : (k + 1) * C, cols] = gather_lanes(tail_ref, index[:, cols])
    preact = jnp.dot(weight_ref[...], picked_ref[...], preferred_element_type=F32)
    logistic = jax.nn.sigmoid(preact)
    out_ref[...] = (preact * logistic).astype(BF)
    slope = logistic * (1.0 + preact * (1.0 - logistic))
    grad_pre = (cot_ref[...].astype(F32) * slope).astype(BF)
    for block in range(V // FORWARD_VB):

        @pl.when(step == block)
        def _(first=block * FORWARD_VB):
            for part, pre_ref in enumerate(pre_refs):
                at = sum(PARTS[:part]) * VB
                low, high = max(first, at), min(first + FORWARD_VB, at + PARTS[part] * VB)
                if low < high:
                    pre_ref[:, low - at : high - at] = grad_pre[:, low - first : high - first]

    acc_ref[...] += lax.dot_general(picked_ref[...], grad_pre, NT, preferred_element_type=F32)

    @pl.when(step == pl.num_programs(0) - 1)
    def _():
        for t in range(TILES + 1):
            block = acc_ref[t * LANES : min((t + 1) * LANES, K * C), :].T
            if t == TILES:
                block = jnp.concatenate([block, jnp.zeros((C, LANES - block.shape[1]), F32)], axis=1)
            block = block.astype(BF)
            for i in range(C // 16):
                shard, slot = tile_place(i, t)
                wg_ref[shard, slot * 16 : (slot + 1) * 16, :] = block[i * 16 : (i + 1) * 16, :]
        used = (TILES + 1) * (C // 16) - (GROUPS - 1) * SHARD_TILES
        wg_ref[GROUPS - 1, used * 16 :, :] = jnp.zeros((LANES - used * 16, LANES), BF)


def forward_pass(owned, low, high, kernel_map, weight, cotangent):
    whole = lambda *shape: pl.BlockSpec(shape, lambda i: (0,) * len(shape))
    column = lambda rows: pl.BlockSpec((rows, FORWARD_VB), lambda i: (0, i))
    return pl.pallas_call(
        forward_kernel,
        grid=(V // FORWARD_VB,),
        in_specs=[
            whole(GROUPS, C, CAP),
            whole(C, F),
            whole(C, F),
            pl.BlockSpec((K, 1, FORWARD_VB), lambda i: (0, 0, i)),
            whole(C, K * C),
            column(C),
        ],
        out_specs=(column(C), *(whole(C, n * VB) for n in PARTS), whole(GROUPS, LANES, LANES)),
        out_shape=(
            jax.ShapeDtypeStruct((C, V), BF),
            *(jax.ShapeDtypeStruct((C, n * VB), BF) for n in PARTS),
            jax.ShapeDtypeStruct((GROUPS, LANES, LANES), BF),
        ),
        scratch_shapes=[
            pltpu.VMEM((WIDE_BANKS * MAIN, WIDE), BF),
            pltpu.VMEM((V // CAP + 2 * F // CAP, C - MAIN, CAP), BF),
            pltpu.VMEM((K * C, FORWARD_VB), BF),
            pltpu.VMEM((K * C, C), F32),
        ],
        compiler_params=pltpu.CompilerParams(vmem_limit_bytes=32 << 20),
        cost_estimate=pl.CostEstimate(
            flops=2 * K * V * ALL_BANKS * C * LO, bytes_accessed=4 << 20, transcendentals=C * V
        ),
        name="gather_forward",
    )(owned, low, high, kernel_map, weight, cotangent)


def bank_rows(values, bank, banks):
    n = bank.shape[-1]
    bank16 = rows16(bank)
    values = values.reshape(C // 16, 16, n)
    return jnp.concatenate([jnp.where((bank16 == a)[None], values, BF(0)).reshape(C, n) for a in banks], axis=0)


def scatter_kernel(banks, has_start, after_ref, start_ref, map_ref, weight_ref, pre_ref, *refs):
    *out_refs, spread_ref, acc_ref = refs

    @pl.when(pl.program_id(0) == 0)
    def _():
        acc_ref[...] = start_ref[...] if has_start else jnp.zeros_like(acc_ref)

    spread_ref[...] = jnp.dot(weight_ref[...], pre_ref[...], preferred_element_type=F32).astype(BF)
    for first in range(0, K, PER_DOT):
        spreads, hots = [], []
        for k in range(first, first + PER_DOT):
            index = map_ref[k]
            spreads.append(bank_rows(spread_ref[k * C : (k + 1) * C, :], index >> 8, banks))
            hots.append(onehot_rows(index & (LO - 1), LO))
        acc_ref[...] += lax.dot_general(
            jnp.concatenate(spreads, axis=1), jnp.concatenate(hots, axis=1), NT, preferred_element_type=F32
        )

    @pl.when(pl.program_id(0) == pl.num_programs(0) - 1)
    def _():
        rows = acc_ref.shape[0] // len(out_refs)
        for i, out_ref in enumerate(out_refs):
            out_ref[...] = acc_ref[i * rows : (i + 1) * rows, :].astype(out_ref.dtype)


def scatter_part(part, banks, after, start, kernel_map, weight, grad_pre, split=1, dtype=F32):
    whole = lambda *shape: pl.BlockSpec(shape, lambda i: (0,) * len(shape))
    rows, at, steps = len(banks) * C, sum(PARTS[:part]), PARTS[part]
    start_spec = pl.BlockSpec((rows, LO), lambda i: (banks[0] // len(banks), 0))
    return pl.pallas_call(
        functools.partial(scatter_kernel, banks, part > 0),
        grid=(steps,),
        in_specs=[
            pl.BlockSpec(memory_space=pl.ANY),
            start_spec if part > 0 else pl.BlockSpec(memory_space=pl.ANY),
            pl.BlockSpec((K, 1, VB), lambda i: (0, 0, at + i)),
            whole(K * C, C),
            pl.BlockSpec((C, VB), lambda i: (0, i)),
        ],
        out_specs=(whole(rows // split, LO),) * split,
        out_shape=(jax.ShapeDtypeStruct((rows // split, LO), dtype),) * split,
        scratch_shapes=[pltpu.VMEM((K * C, VB), BF), pltpu.VMEM((rows, LO), F32)],
        compiler_params=pltpu.CompilerParams(vmem_limit_bytes=24 << 20),
        cost_estimate=pl.CostEstimate(
            flops=2 * K * VB * steps * rows * LO, bytes_accessed=2 << 20, transcendentals=0
        ),
        name="scatter",
    )(after, start, kernel_map, weight, grad_pre[part])


def total_of(parts_ref):
    total = parts_ref[0].astype(F32)
    for g in range(1, GROUPS):
        total = total + parts_ref[g].astype(F32)
    return total.astype(BF)


def sum_parts_kernel(after_ref, parts_ref, out_ref):
    total = total_of(parts_ref)
    for g in range(GROUPS):
        out_ref[g] = total


def sum_parts(after, parts):
    return pl.pallas_call(
        sum_parts_kernel,
        in_specs=[pl.BlockSpec(memory_space=pl.ANY), pl.BlockSpec(memory_space=pltpu.VMEM)],
        out_shape=jax.ShapeDtypeStruct(parts.shape, BF),
        compiler_params=pltpu.CompilerParams(vmem_limit_bytes=8 << 20),
        name="sum_parts",
    )(after, parts)


def fold_kernel(grad_ref, from_low_ref, from_high_ref, rows_ref, parts_ref, out_ref, masked_ref):
    share = total_of(parts_ref)
    hots = []
    for j, part_ref in enumerate((from_low_ref, from_high_ref)):
        rows = rows_ref[j : j + 1, :]
        masked_banks(part_ref[...], rows >> 8, BANKS, masked_ref, j * F)
        hots.append(onehot_rows(rows & (LO - 1), LO))
    folded = lax.dot_general(
        masked_ref[...], jnp.concatenate(hots, axis=1), NT, preferred_element_type=F32
    )
    total = (grad_ref[...] + folded).astype(BF)
    for g in range(GROUPS):
        out_ref[g, :C, :] = total[(g // 2) * C : (g // 2 + 1) * C, (g % 2) * CAP : (g % 2 + 1) * CAP]
        out_ref[g, C:, :] = share


def fold_faces(table_grad, from_low, from_high, face_rows, parts):
    return pl.pallas_call(
        fold_kernel,
        out_shape=jax.ShapeDtypeStruct((GROUPS, C + LANES, CAP), BF),
        scratch_shapes=[pltpu.VMEM((BANKS * C, 2 * F), BF)],
        compiler_params=pltpu.CompilerParams(vmem_limit_bytes=16 << 20),
        name="fold",
    )(table_grad, from_low, from_high, face_rows, parts)


def finish_kernel(scale, back_ref, owner_ref, slot_ref, out_ref, wg_ref, flat_ref):
    table = back_ref[:, :C, :].reshape(GROUPS * C, CAP)
    for b in range(R // LO):
        cols = slice(b * LO, (b + 1) * LO)
        product = jnp.dot(table, onehot_rows(slot_ref[:, cols], CAP), preferred_element_type=F32)
        out_ref[:, cols] = select_banks(product, owner_ref[:, cols], GROUPS).astype(BF)
    for t in range(TILES + 1):
        for i in range(C // 16):
            shard, slot = tile_place(i, t)
            tile = back_ref[shard, C + slot * 16 : C + (slot + 1) * 16, :].astype(F32) * scale
            flat_ref[i * 16 : (i + 1) * 16, t * LANES : (t + 1) * LANES] = tile
    for k in range(K):
        wg_ref[k] = flat_ref[:, k * C : (k + 1) * C]


def finish(returned, owner, slot, scale):
    return pl.pallas_call(
        functools.partial(finish_kernel, scale),
        out_shape=(jax.ShapeDtypeStruct((C, R), BF), jax.ShapeDtypeStruct((K, C, C), F32)),
        scratch_shapes=[pltpu.VMEM((C, (TILES + 1) * LANES), F32)],
        compiler_params=pltpu.CompilerParams(vmem_limit_bytes=24 << 20),
        name="finish",
    )(returned, owner, slot)


def body(points, owners, kernel_maps, face_rows, weight, cotangent):
    points, owner = points[0, 0], owners.reshape(1, R)
    kernel_map, face_list, incoming = kernel_maps.reshape(K, 1, V), face_rows[0, 0], cotangent[0, 0]
    side = lax.axis_size("sy")
    up = [(i, i + 1) for i in range(side - 1)]
    down = [(i + 1, i) for i in range(side - 1)]

    outgoing, slot = place_points(points, owner)
    owned = lax.all_to_all(outgoing, "sx", 0, 0, tiled=True)
    lower, upper = take_faces(owned, face_list)
    ghost_low = lax.ppermute(upper, "sy", up)
    ghost_high = lax.ppermute(lower, "sy", down)
    weight_rows = jnp.transpose(weight, (1, 0, 2)).reshape(C, K * C)
    output, *grad_pre, weight_part = forward_pass(
        owned, ghost_low, ghost_high, kernel_map, weight_rows, incoming
    )
    weight_columns = jnp.transpose(weight, (0, 2, 1)).reshape(K * C, C)
    scatter = functools.partial(scatter_part, kernel_map=kernel_map, weight=weight_columns, grad_pre=grad_pre)
    across = lambda array, axis: lax.all_to_all(array, axis, 0, 0, tiled=True)
    every = range(ALL_BANKS)
    parts = across(weight_part, "sx")
    (sums,) = scatter(0, every, grad_pre[0], grad_pre[0])
    row_sums = sum_parts(sums, parts)
    parts = across(row_sums, "sy")
    (sums,) = scatter(1, every, row_sums, sums)
    to_low, to_high = scatter(2, every[BANKS:], parts, sums, split=2, dtype=BF)
    (table_grad,) = scatter(2, every[:BANKS], to_low, sums)
    from_low = lax.ppermute(to_high, "sy", up)
    from_high = lax.ppermute(to_low, "sy", down)
    owned_grad = fold_faces(table_grad, from_low, from_high, face_list, parts)
    returned = across(owned_grad, "sx")
    scale = 1.0 / math.sqrt(GROUPS * side * V)
    point_grad, weight_grad = finish(returned, owner, slot, scale)
    return (output[None, None], point_grad[None, None], weight_grad)


def solution(mesh):
    split = P("sx", "sy", None, None)
    return jax.shard_map(
        body,
        mesh=mesh,
        in_specs=(split, split, split, split, P(), split),
        out_specs=(split, split, P()),
        check_vma=False,
    )
```

```python
import functools
import math

import jax
import jax.numpy as jnp
from jax import lax
from jax.experimental import pallas as pl
from jax.experimental.pallas import tpu as pltpu
from jax.sharding import PartitionSpec as P

C = 96
K = 27
R = 1024
F = 256
CAP = 128
V = 2048
GROUPS = 16
LO = 256
BANKS = V // LO
ALL_BANKS = BANKS + 2
WIDE = 512
WIDE_BANKS = ALL_BANKS * LO // WIDE
VB = 256
FORWARD_VB = 512
MAIN = 64
PER_DOT = 3
PARTS = (3, 3, 2)
LANES = 128
TILES = K * C // LANES
SHARD_TILES = 8

BF = jnp.bfloat16
F32 = jnp.float32
NT = (((1,), (1,)), ((), ()))


def rows16(index):
    return jnp.broadcast_to(index, (16, index.shape[-1])).astype(jnp.int16)


def onehot_rows(low, rows):
    n = low.shape[-1]
    row = lax.broadcasted_iota(jnp.int16, (rows, n), 0).reshape(rows // 16, 16, n)
    return jnp.where(row == rows16(low)[None], BF(1), BF(0)).reshape(rows, n)


def select_banks(product, bank, banks, channels=C):
    n = bank.shape[-1]
    bank8 = jnp.broadcast_to(bank, (8, n))
    kept = jnp.zeros((channels // 8, 8, n), F32)
    for a in range(banks):
        part = product[a * channels : (a + 1) * channels].reshape(channels // 8, 8, n)
        kept = jnp.where((bank8 == a)[None], part, kept)
    return kept.reshape(channels, n)


LANE_GATHER = lax.GatherDimensionNumbers(
    offset_dims=(),
    collapsed_slice_dims=(1,),
    start_index_map=(1,),
    operand_batching_dims=(0,),
    start_indices_batching_dims=(0,),
)


def gather_lanes(tiles_ref, index):
    tiles, rows, _ = tiles_ref.shape
    lane, tile = rows16(index & (CAP - 1)), rows16(index >> 7)
    kept = [jnp.zeros((16, CAP), BF) for _ in range(rows // 16)]
    for t in range(tiles):
        mine = tile == t
        for h in range(rows // 16):
            read = lax.gather(
                tiles_ref[t, h * 16 : (h + 1) * 16, :],
                lane[..., None],
                LANE_GATHER,
                (1, 1),
                mode=lax.GatherScatterMode.PROMISE_IN_BOUNDS,
            )
            kept[h] = jnp.where(mine, read, kept[h])
    return jnp.concatenate(kept, axis=0)


def masked_banks(values, bank, banks, out_ref, column):
    n = bank.shape[-1]
    bank16 = rows16(bank)
    values = values.reshape(C // 16, 16, n)
    for a in range(banks):
        spread = jnp.where((bank16 == a)[None], values, BF(0))
        out_ref[a * C : (a + 1) * C, column : column + n] = spread.reshape(C, n)


def tile_place(i, t):
    return divmod(i * TILES + t if t < TILES else (C // 16) * TILES + i, SHARD_TILES)


def place_kernel(points_ref, owner_ref, out_ref, slot_ref, masked_ref):
    owner = owner_ref[...]
    row = lax.broadcasted_iota(jnp.int32, (CAP, CAP), 0)
    col = lax.broadcasted_iota(jnp.int32, (CAP, CAP), 1)
    earlier = jnp.where(row < col, 1.0, 0.0).astype(BF)
    group = lax.broadcasted_iota(jnp.int32, (GROUPS, CAP), 0)
    total = jnp.zeros((GROUPS, 1), F32)
    for b in range(R // CAP):
        mine = jnp.where(group == owner[:, b * CAP : (b + 1) * CAP], 1.0, 0.0)
        before = jnp.dot(mine.astype(BF), earlier, preferred_element_type=F32) + total
        slot = jnp.sum(mine * before, axis=0, keepdims=True)
        slot_ref[:, b * CAP : (b + 1) * CAP] = slot.astype(jnp.int32)
        total = total + jnp.sum(mine, axis=1, keepdims=True)
    masked_banks(points_ref[...], owner, GROUPS, masked_ref, 0)
    onehot = onehot_rows(slot_ref[...], CAP)
    for g in range(GROUPS):
        out_ref[g] = lax.dot_general(
            masked_ref[g * C : (g + 1) * C, :], onehot, NT, preferred_element_type=F32
        ).astype(BF)


def place_points(points, owner):
    return pl.pallas_call(
        place_kernel,
        out_shape=(
            jax.ShapeDtypeStruct((GROUPS, C, CAP), BF),
            jax.ShapeDtypeStruct((1, R), jnp.int32),
        ),
        scratch_shapes=[pltpu.VMEM((GROUPS * C, R), BF)],
        compiler_params=pltpu.CompilerParams(vmem_limit_bytes=16 << 20),
        name="place",
    )(points, owner)


def faces_kernel(owned_ref, rows_ref, lower_ref, upper_ref):
    table = owned_ref[...].reshape(GROUPS * C, CAP)
    for j, out_ref in enumerate((lower_ref, upper_ref)):
        rows = rows_ref[j : j + 1, :]
        product = jnp.dot(table, onehot_rows(rows & (CAP - 1), CAP), preferred_element_type=F32)
        out_ref[...] = select_banks(product, rows >> 7, GROUPS).astype(BF)


def take_faces(owned, face_rows):
    return pl.pallas_call(
        faces_kernel,
        out_shape=(jax.ShapeDtypeStruct((C, F), BF),) * 2,
        compiler_params=pltpu.CompilerParams(vmem_limit_bytes=16 << 20),
        name="faces",
    )(owned, face_rows)


def forward_kernel(
    owned_ref, low_ref, high_ref, map_ref, weight_ref, cot_ref, out_ref, *refs
):
    pre_refs, (wg_ref, table_ref, tail_ref, picked_ref, acc_ref) = refs[: len(PARTS)], refs[len(PARTS) :]
    step = pl.program_id(0)

    @pl.when(step == 0)
    def _():
        per = WIDE // CAP
        for g in range(GROUPS):
            rows = slice((g // per) * MAIN, (g // per + 1) * MAIN)
            table_ref[rows, (g % per) * CAP : (g % per + 1) * CAP] = owned_ref[g, :MAIN, :]
            tail_ref[g] = owned_ref[g, MAIN:, :]
        for j, ghost_ref in enumerate((low_ref, high_ref)):
            bank, at = divmod(V + j * F, WIDE)
            table_ref[bank * MAIN : (bank + 1) * MAIN, at : at + F] = ghost_ref[:MAIN, :]
            for i in range(F // CAP):
                tail_ref[GROUPS + j * (F // CAP) + i] = ghost_ref[MAIN:, i * CAP : (i + 1) * CAP]
        acc_ref[...] = jnp.zeros_like(acc_ref)

    table = table_ref[...]
    for k in range(K):
        index = map_ref[k]
        product = jnp.dot(table, onehot_rows(index & (WIDE - 1), WIDE), preferred_element_type=F32)
        main = select_banks(product, index >> (WIDE.bit_length() - 1), WIDE_BANKS, MAIN)
        picked_ref[k * C : k * C + MAIN, :] = main.astype(BF)
        for i in range(FORWARD_VB // CAP):
            cols = slice(i * CAP, (i + 1) * CAP)
            picked_ref[k * C + MAIN : (k + 1) * C, cols] = gather_lanes(tail_ref, index[:, cols])
    preact = jnp.dot(weight_ref[...], picked_ref[...], preferred_element_type=F32)
    logistic = jax.nn.sigmoid(preact)
    out_ref[...] = (preact * logistic).astype(BF)
    slope = logistic * (1.0 + preact * (1.0 - logistic))
    grad_pre = (cot_ref[...].astype(F32) * slope).astype(BF)
    for block in range(V // FORWARD_VB):

        @pl.when(step == block)
        def _(first=block * FORWARD_VB):
            for part, pre_ref in enumerate(pre_refs):
                at = sum(PARTS[:part]) * VB
                low, high = max(first, at), min(first + FORWARD_VB, at + PARTS[part] * VB)
                if low < high:
                    pre_ref[:, low - at : high - at] = grad_pre[:, low - first : high - first]

    acc_ref[...] += lax.dot_general(picked_ref[...], grad_pre, NT, preferred_element_type=F32)

    @pl.when(step == pl.num_programs(0) - 1)
    def _():
        for t in range(TILES + 1):
            block = acc_ref[t * LANES : min((t + 1) * LANES, K * C), :].T
            if t == TILES:
                block = jnp.concatenate([block, jnp.zeros((C, LANES - block.shape[1]), F32)], axis=1)
            block = block.astype(BF)
            for i in range(C // 16):
                shard, slot = tile_place(i, t)
                wg_ref[shard, slot * 16 : (slot + 1) * 16, :] = block[i * 16 : (i + 1) * 16, :]
        used = (TILES + 1) * (C // 16) - (GROUPS - 1) * SHARD_TILES
        wg_ref[GROUPS - 1, used * 16 :, :] = jnp.zeros((LANES - used * 16, LANES), BF)


def forward_pass(owned, low, high, kernel_map, weight, cotangent):
    whole = lambda *shape: pl.BlockSpec(shape, lambda i: (0,) * len(shape))
    column = lambda rows: pl.BlockSpec((rows, FORWARD_VB), lambda i: (0, i))
    return pl.pallas_call(
        forward_kernel,
        grid=(V // FORWARD_VB,),
        in_specs=[
            whole(GROUPS, C, CAP),
            whole(C, F),
            whole(C, F),
            pl.BlockSpec((K, 1, FORWARD_VB), lambda i: (0, 0, i)),
            whole(C, K * C),
            column(C),
        ],
        out_specs=(column(C), *(whole(C, n * VB) for n in PARTS), whole(GROUPS, LANES, LANES)),
        out_shape=(
            jax.ShapeDtypeStruct((C, V), BF),
            *(jax.ShapeDtypeStruct((C, n * VB), BF) for n in PARTS),
            jax.ShapeDtypeStruct((GROUPS, LANES, LANES), BF),
        ),
        scratch_shapes=[
            pltpu.VMEM((WIDE_BANKS * MAIN, WIDE), BF),
            pltpu.VMEM((V // CAP + 2 * F // CAP, C - MAIN, CAP), BF),
            pltpu.VMEM((K * C, FORWARD_VB), BF),
            pltpu.VMEM((K * C, C), F32),
        ],
        compiler_params=pltpu.CompilerParams(vmem_limit_bytes=32 << 20),
        cost_estimate=pl.CostEstimate(
            flops=2 * K * V * ALL_BANKS * C * LO, bytes_accessed=4 << 20, transcendentals=C * V
        ),
        name="gather_forward",
    )(owned, low, high, kernel_map, weight, cotangent)


def bank_rows(values, bank, banks):
    n = bank.shape[-1]
    bank16 = rows16(bank)
    values = values.reshape(C // 16, 16, n)
    return jnp.concatenate([jnp.where((bank16 == a)[None], values, BF(0)).reshape(C, n) for a in banks], axis=0)


def scatter_kernel(has_start, after_ref, start_ref, map_ref, weight_ref, pre_ref, *refs):
    *out_refs, spread_ref, acc_ref = refs

    @pl.when(pl.program_id(0) == 0)
    def _():
        acc_ref[...] = start_ref[...] if has_start else jnp.zeros_like(acc_ref)

    spread_ref[...] = jnp.dot(weight_ref[...], pre_ref[...], preferred_element_type=F32).astype(BF)
    for first in range(0, K, PER_DOT):
        spreads, hots = [], []
        for k in range(first, first + PER_DOT):
            index = map_ref[k]
            spreads.append(bank_rows(spread_ref[k * C : (k + 1) * C, :], index >> 8, range(ALL_BANKS)))
            hots.append(onehot_rows(index & (LO - 1), LO))
        acc_ref[...] += lax.dot_general(
            jnp.concatenate(spreads, axis=1), jnp.concatenate(hots, axis=1), NT, preferred_element_type=F32
        )

    @pl.when(pl.program_id(0) == pl.num_programs(0) - 1)
    def _():
        at = 0
        for out_ref in out_refs:
            rows = out_ref.shape[0]
            out_ref[...] = acc_ref[at : at + rows, :].astype(out_ref.dtype)
            at += rows


def scatter_part(part, after, start, kernel_map, weight, grad_pre):
    whole = lambda *shape: pl.BlockSpec(shape, lambda i: (0,) * len(shape))
    rows, at, steps = ALL_BANKS * C, sum(PARTS[:part]), PARTS[part]
    outs = [(rows, F32)] if part < len(PARTS) - 1 else [(BANKS * C, F32), (C, BF), (C, BF)]
    return pl.pallas_call(
        functools.partial(scatter_kernel, part > 0),
        grid=(steps,),
        in_specs=[
            pl.BlockSpec(memory_space=pl.ANY),
            whole(rows, LO) if part > 0 else pl.BlockSpec(memory_space=pl.ANY),
            pl.BlockSpec((K, 1, VB), lambda i: (0, 0, at + i)),
            whole(K * C, C),
            pl.BlockSpec((C, VB), lambda i: (0, i)),
        ],
        out_specs=tuple(whole(n, LO) for n, _ in outs),
        out_shape=tuple(jax.ShapeDtypeStruct((n, LO), dtype) for n, dtype in outs),
        scratch_shapes=[pltpu.VMEM((K * C, VB), BF), pltpu.VMEM((rows, LO), F32)],
        compiler_params=pltpu.CompilerParams(vmem_limit_bytes=24 << 20),
        cost_estimate=pl.CostEstimate(
            flops=2 * K * VB * steps * rows * LO, bytes_accessed=2 << 20, transcendentals=0
        ),
        name="scatter",
    )(after, start, kernel_map, weight, grad_pre[part])


def total_of(parts_ref):
    total = parts_ref[0].astype(F32)
    for g in range(1, GROUPS):
        total = total + parts_ref[g].astype(F32)
    return total.astype(BF)


def sum_parts_kernel(after_ref, parts_ref, out_ref):
    total = total_of(parts_ref)
    for g in range(GROUPS):
        out_ref[g] = total


def sum_parts(after, parts):
    return pl.pallas_call(
        sum_parts_kernel,
        in_specs=[pl.BlockSpec(memory_space=pl.ANY), pl.BlockSpec(memory_space=pltpu.VMEM)],
        out_shape=jax.ShapeDtypeStruct(parts.shape, BF),
        compiler_params=pltpu.CompilerParams(vmem_limit_bytes=8 << 20),
        name="sum_parts",
    )(after, parts)


def fold_kernel(grad_ref, from_low_ref, from_high_ref, rows_ref, parts_ref, out_ref, masked_ref):
    share = total_of(parts_ref)
    hots = []
    for j, part_ref in enumerate((from_low_ref, from_high_ref)):
        rows = rows_ref[j : j + 1, :]
        masked_banks(part_ref[...], rows >> 8, BANKS, masked_ref, j * F)
        hots.append(onehot_rows(rows & (LO - 1), LO))
    folded = lax.dot_general(
        masked_ref[...], jnp.concatenate(hots, axis=1), NT, preferred_element_type=F32
    )
    total = (grad_ref[...] + folded).astype(BF)
    for g in range(GROUPS):
        out_ref[g, :C, :] = total[(g // 2) * C : (g // 2 + 1) * C, (g % 2) * CAP : (g % 2 + 1) * CAP]
        out_ref[g, C:, :] = share


def fold_faces(table_grad, from_low, from_high, face_rows, parts):
    return pl.pallas_call(
        fold_kernel,
        out_shape=jax.ShapeDtypeStruct((GROUPS, C + LANES, CAP), BF),
        scratch_shapes=[pltpu.VMEM((BANKS * C, 2 * F), BF)],
        compiler_params=pltpu.CompilerParams(vmem_limit_bytes=16 << 20),
        name="fold",
    )(table_grad, from_low, from_high, face_rows, parts)


def finish_kernel(scale, back_ref, owner_ref, slot_ref, out_ref, wg_ref, flat_ref):
    table = back_ref[:, :C, :].reshape(GROUPS * C, CAP)
    for b in range(R // LO):
        cols = slice(b * LO, (b + 1) * LO)
        product = jnp.dot(table, onehot_rows(slot_ref[:, cols], CAP), preferred_element_type=F32)
        out_ref[:, cols] = select_banks(product, owner_ref[:, cols], GROUPS).astype(BF)
    for t in range(TILES + 1):
        for i in range(C // 16):
            shard, slot = tile_place(i, t)
            tile = back_ref[shard, C + slot * 16 : C + (slot + 1) * 16, :].astype(F32) * scale
            flat_ref[i * 16 : (i + 1) * 16, t * LANES : (t + 1) * LANES] = tile
    for k in range(K):
        wg_ref[k] = flat_ref[:, k * C : (k + 1) * C]


def finish(returned, owner, slot, scale):
    return pl.pallas_call(
        functools.partial(finish_kernel, scale),
        out_shape=(jax.ShapeDtypeStruct((C, R), BF), jax.ShapeDtypeStruct((K, C, C), F32)),
        scratch_shapes=[pltpu.VMEM((C, (TILES + 1) * LANES), F32)],
        compiler_params=pltpu.CompilerParams(vmem_limit_bytes=24 << 20),
        name="finish",
    )(returned, owner, slot)


def body(points, owners, kernel_maps, face_rows, weight, cotangent):
    points, owner = points[0, 0], owners.reshape(1, R)
    kernel_map, face_list, incoming = kernel_maps.reshape(K, 1, V), face_rows[0, 0], cotangent[0, 0]
    side = lax.axis_size("sy")
    up = [(i, i + 1) for i in range(side - 1)]
    down = [(i + 1, i) for i in range(side - 1)]

    outgoing, slot = place_points(points, owner)
    owned = lax.all_to_all(outgoing, "sx", 0, 0, tiled=True)
    lower, upper = take_faces(owned, face_list)
    ghost_low = lax.ppermute(upper, "sy", up)
    ghost_high = lax.ppermute(lower, "sy", down)
    weight_rows = jnp.transpose(weight, (1, 0, 2)).reshape(C, K * C)
    output, *grad_pre, weight_part = forward_pass(
        owned, ghost_low, ghost_high, kernel_map, weight_rows, incoming
    )
    weight_columns = jnp.transpose(weight, (0, 2, 1)).reshape(K * C, C)
    scatter = functools.partial(scatter_part, kernel_map=kernel_map, weight=weight_columns, grad_pre=grad_pre)
    across = lambda array, axis: lax.all_to_all(array, axis, 0, 0, tiled=True)
    parts = across(weight_part, "sx")
    (sums,) = scatter(0, grad_pre[0], grad_pre[0])
    row_sums = sum_parts(sums, parts)
    parts = across(row_sums, "sy")
    (sums,) = scatter(1, row_sums, sums)
    table_grad, to_low, to_high = scatter(2, parts, sums)
    from_low = lax.ppermute(to_high, "sy", up)
    from_high = lax.ppermute(to_low, "sy", down)
    owned_grad = fold_faces(table_grad, from_low, from_high, face_list, parts)
    returned = across(owned_grad, "sx")
    scale = 1.0 / math.sqrt(GROUPS * side * V)
    point_grad, weight_grad = finish(returned, owner, slot, scale)
    return (output[None, None], point_grad[None, None], weight_grad)


def solution(mesh):
    split = P("sx", "sy", None, None)
    return jax.shard_map(
        body,
        mesh=mesh,
        in_specs=(split, split, split, split, P(), split),
        out_specs=(split, split, P()),
        check_vma=False,
    )
```

```python
import functools
import math

import jax
import jax.numpy as jnp
from jax import lax
from jax.experimental import pallas as pl
from jax.experimental.pallas import tpu as pltpu
from jax.sharding import PartitionSpec as P

C = 96
K = 27
R = 1024
F = 256
CAP = 128
V = 2048
GROUPS = 16
LO = 256
BANKS = V // LO
ALL_BANKS = BANKS + 2
WIDE = 512
WIDE_BANKS = ALL_BANKS * LO // WIDE
VB = 256
FORWARD_VB = 512
MAIN = 64
PER_DOT = 3
PARTS = (3, 3, 2)
LANES = 128
TILES = K * C // LANES
SHARD_TILES = 8

BF = jnp.bfloat16
F32 = jnp.float32
NT = (((1,), (1,)), ((), ()))


def rows16(index):
    return jnp.broadcast_to(index, (16, index.shape[-1])).astype(jnp.int16)


def onehot_rows(low, rows):
    n = low.shape[-1]
    row = lax.broadcasted_iota(jnp.int16, (rows, n), 0).reshape(rows // 16, 16, n)
    return jnp.where(row == rows16(low)[None], BF(1), BF(0)).reshape(rows, n)


def select_banks(product, bank, banks, channels=C):
    n = bank.shape[-1]
    bank8 = jnp.broadcast_to(bank, (8, n))
    kept = jnp.zeros((channels // 8, 8, n), F32)
    for a in range(banks):
        part = product[a * channels : (a + 1) * channels].reshape(channels // 8, 8, n)
        kept = jnp.where((bank8 == a)[None], part, kept)
    return kept.reshape(channels, n)


LANE_GATHER = lax.GatherDimensionNumbers(
    offset_dims=(),
    collapsed_slice_dims=(1,),
    start_index_map=(1,),
    operand_batching_dims=(0,),
    start_indices_batching_dims=(0,),
)


def gather_lanes(tiles_ref, index):
    tiles, rows, _ = tiles_ref.shape
    lane, tile = rows16(index & (CAP - 1)), rows16(index >> 7)
    kept = [jnp.zeros((16, CAP), BF) for _ in range(rows // 16)]
    for t in range(tiles):
        mine = tile == t
        for h in range(rows // 16):
            read = lax.gather(
                tiles_ref[t, h * 16 : (h + 1) * 16, :],
                lane[..., None],
                LANE_GATHER,
                (1, 1),
                mode=lax.GatherScatterMode.PROMISE_IN_BOUNDS,
            )
            kept[h] = jnp.where(mine, read, kept[h])
    return jnp.concatenate(kept, axis=0)


def masked_banks(values, bank, banks, out_ref, column):
    n = bank.shape[-1]
    bank16 = rows16(bank)
    values = values.reshape(C // 16, 16, n)
    for a in range(banks):
        spread = jnp.where((bank16 == a)[None], values, BF(0))
        out_ref[a * C : (a + 1) * C, column : column + n] = spread.reshape(C, n)


def tile_place(i, t):
    return divmod(i * TILES + t if t < TILES else (C // 16) * TILES + i, SHARD_TILES)


def place_kernel(points_ref, lists_ref, out_ref, slot_ref, masked_ref):
    owner = lists_ref[:, :R]
    row = lax.broadcasted_iota(jnp.int32, (CAP, CAP), 0)
    col = lax.broadcasted_iota(jnp.int32, (CAP, CAP), 1)
    earlier = jnp.where(row < col, 1.0, 0.0).astype(BF)
    group = lax.broadcasted_iota(jnp.int32, (GROUPS, CAP), 0)
    total = jnp.zeros((GROUPS, 1), F32)
    for b in range(R // CAP):
        mine = jnp.where(group == owner[:, b * CAP : (b + 1) * CAP], 1.0, 0.0)
        before = jnp.dot(mine.astype(BF), earlier, preferred_element_type=F32) + total
        slot = jnp.sum(mine * before, axis=0, keepdims=True)
        slot_ref[:, b * CAP : (b + 1) * CAP] = slot.astype(jnp.int32)
        total = total + jnp.sum(mine, axis=1, keepdims=True)
    masked_banks(points_ref[...], owner, GROUPS, masked_ref, 0)
    onehot = onehot_rows(slot_ref[...], CAP)
    for g in range(GROUPS):
        out_ref[g] = lax.dot_general(
            masked_ref[g * C : (g + 1) * C, :], onehot, NT, preferred_element_type=F32
        ).astype(BF)


def place_points(points, lists):
    return pl.pallas_call(
        place_kernel,
        out_shape=(
            jax.ShapeDtypeStruct((GROUPS, C, CAP), BF),
            jax.ShapeDtypeStruct((1, R), jnp.int32),
        ),
        scratch_shapes=[pltpu.VMEM((GROUPS * C, R), BF)],
        compiler_params=pltpu.CompilerParams(vmem_limit_bytes=16 << 20),
        name="place",
    )(points, lists)


def faces_kernel(owned_ref, lists_ref, lower_ref, upper_ref):
    table = owned_ref[...].reshape(GROUPS * C, CAP)
    for j, out_ref in enumerate((lower_ref, upper_ref)):
        rows = lists_ref[:, R + j * F : R + (j + 1) * F]
        product = jnp.dot(table, onehot_rows(rows & (CAP - 1), CAP), preferred_element_type=F32)
        out_ref[...] = select_banks(product, rows >> 7, GROUPS).astype(BF)


def take_faces(owned, lists):
    return pl.pallas_call(
        faces_kernel,
        out_shape=(jax.ShapeDtypeStruct((C, F), BF),) * 2,
        compiler_params=pltpu.CompilerParams(vmem_limit_bytes=16 << 20),
        name="faces",
    )(owned, lists)


def forward_kernel(
    owned_ref, low_ref, high_ref, map_ref, weight_ref, cot_ref, out_ref, *refs
):
    pre_refs, (wg_ref, table_ref, tail_ref, picked_ref, acc_ref) = refs[: len(PARTS)], refs[len(PARTS) :]
    step = pl.program_id(0)

    @pl.when(step == 0)
    def _():
        per = WIDE // CAP
        for g in range(GROUPS):
            rows = slice((g // per) * MAIN, (g // per + 1) * MAIN)
            table_ref[rows, (g % per) * CAP : (g % per + 1) * CAP] = owned_ref[g, :MAIN, :]
            tail_ref[g] = owned_ref[g, MAIN:, :]
        for j, ghost_ref in enumerate((low_ref, high_ref)):
            bank, at = divmod(V + j * F, WIDE)
            table_ref[bank * MAIN : (bank + 1) * MAIN, at : at + F] = ghost_ref[:MAIN, :]
            for i in range(F // CAP):
                tail_ref[GROUPS + j * (F // CAP) + i] = ghost_ref[MAIN:, i * CAP : (i + 1) * CAP]
        acc_ref[...] = jnp.zeros_like(acc_ref)

    table = table_ref[...]
    for k in range(K):
        index = map_ref[k]
        product = jnp.dot(table, onehot_rows(index & (WIDE - 1), WIDE), preferred_element_type=F32)
        main = select_banks(product, index >> (WIDE.bit_length() - 1), WIDE_BANKS, MAIN)
        picked_ref[k * C : k * C + MAIN, :] = main.astype(BF)
        for i in range(FORWARD_VB // CAP):
            cols = slice(i * CAP, (i + 1) * CAP)
            picked_ref[k * C + MAIN : (k + 1) * C, cols] = gather_lanes(tail_ref, index[:, cols])
    preact = jnp.dot(weight_ref[...], picked_ref[...], preferred_element_type=F32)
    logistic = jax.nn.sigmoid(preact)
    out_ref[...] = (preact * logistic).astype(BF)
    slope = logistic * (1.0 + preact * (1.0 - logistic))
    grad_pre = (cot_ref[...].astype(F32) * slope).astype(BF)
    for block in range(V // FORWARD_VB):

        @pl.when(step == block)
        def _(first=block * FORWARD_VB):
            for part, pre_ref in enumerate(pre_refs):
                at = sum(PARTS[:part]) * VB
                low, high = max(first, at), min(first + FORWARD_VB, at + PARTS[part] * VB)
                if low < high:
                    pre_ref[:, low - at : high - at] = grad_pre[:, low - first : high - first]

    acc_ref[...] += lax.dot_general(picked_ref[...], grad_pre, NT, preferred_element_type=F32)

    @pl.when(step == pl.num_programs(0) - 1)
    def _():
        for t in range(TILES + 1):
            block = acc_ref[t * LANES : min((t + 1) * LANES, K * C), :].T
            if t == TILES:
                block = jnp.concatenate([block, jnp.zeros((C, LANES - block.shape[1]), F32)], axis=1)
            block = block.astype(BF)
            for i in range(C // 16):
                shard, slot = tile_place(i, t)
                wg_ref[shard, slot * 16 : (slot + 1) * 16, :] = block[i * 16 : (i + 1) * 16, :]
        used = (TILES + 1) * (C // 16) - (GROUPS - 1) * SHARD_TILES
        wg_ref[GROUPS - 1, used * 16 :, :] = jnp.zeros((LANES - used * 16, LANES), BF)


def forward_pass(owned, low, high, kernel_map, weight, cotangent):
    whole = lambda *shape: pl.BlockSpec(shape, lambda i: (0,) * len(shape))
    column = lambda rows: pl.BlockSpec((rows, FORWARD_VB), lambda i: (0, i))
    return pl.pallas_call(
        forward_kernel,
        grid=(V // FORWARD_VB,),
        in_specs=[
            whole(GROUPS, C, CAP),
            whole(C, F),
            whole(C, F),
            pl.BlockSpec((K, 1, FORWARD_VB), lambda i: (0, 0, i)),
            whole(C, K * C),
            column(C),
        ],
        out_specs=(column(C), *(whole(C, n * VB) for n in PARTS), whole(GROUPS, LANES, LANES)),
        out_shape=(
            jax.ShapeDtypeStruct((C, V), BF),
            *(jax.ShapeDtypeStruct((C, n * VB), BF) for n in PARTS),
            jax.ShapeDtypeStruct((GROUPS, LANES, LANES), BF),
        ),
        scratch_shapes=[
            pltpu.VMEM((WIDE_BANKS * MAIN, WIDE), BF),
            pltpu.VMEM((V // CAP + 2 * F // CAP, C - MAIN, CAP), BF),
            pltpu.VMEM((K * C, FORWARD_VB), BF),
            pltpu.VMEM((K * C, C), F32),
        ],
        compiler_params=pltpu.CompilerParams(vmem_limit_bytes=32 << 20),
        cost_estimate=pl.CostEstimate(
            flops=2 * K * V * ALL_BANKS * C * LO, bytes_accessed=4 << 20, transcendentals=C * V
        ),
        name="gather_forward",
    )(owned, low, high, kernel_map, weight, cotangent)


def bank_rows(values, bank, banks):
    n = bank.shape[-1]
    bank16 = rows16(bank)
    values = values.reshape(C // 16, 16, n)
    return jnp.concatenate([jnp.where((bank16 == a)[None], values, BF(0)).reshape(C, n) for a in banks], axis=0)


def scatter_kernel(has_start, after_ref, start_ref, map_ref, weight_ref, pre_ref, *refs):
    *out_refs, spread_ref, acc_ref = refs

    @pl.when(pl.program_id(0) == 0)
    def _():
        acc_ref[...] = start_ref[...] if has_start else jnp.zeros_like(acc_ref)

    spread_ref[...] = jnp.dot(weight_ref[...], pre_ref[...], preferred_element_type=F32).astype(BF)
    for first in range(0, K, PER_DOT):
        spreads, hots = [], []
        for k in range(first, first + PER_DOT):
            index = map_ref[k]
            spreads.append(bank_rows(spread_ref[k * C : (k + 1) * C, :], index >> 8, range(ALL_BANKS)))
            hots.append(onehot_rows(index & (LO - 1), LO))
        acc_ref[...] += lax.dot_general(
            jnp.concatenate(spreads, axis=1), jnp.concatenate(hots, axis=1), NT, preferred_element_type=F32
        )

    @pl.when(pl.program_id(0) == pl.num_programs(0) - 1)
    def _():
        at = 0
        for out_ref in out_refs:
            rows = out_ref.shape[0]
            out_ref[...] = acc_ref[at : at + rows, :].astype(out_ref.dtype)
            at += rows


def scatter_part(part, after, start, kernel_map, weight, grad_pre):
    whole = lambda *shape: pl.BlockSpec(shape, lambda i: (0,) * len(shape))
    rows, at, steps = ALL_BANKS * C, sum(PARTS[:part]), PARTS[part]
    outs = [(rows, F32)] if part < len(PARTS) - 1 else [(BANKS * C, F32), (C, BF), (C, BF)]
    return pl.pallas_call(
        functools.partial(scatter_kernel, part > 0),
        grid=(steps,),
        in_specs=[
            pl.BlockSpec(memory_space=pl.ANY),
            whole(rows, LO) if part > 0 else pl.BlockSpec(memory_space=pl.ANY),
            pl.BlockSpec((K, 1, VB), lambda i: (0, 0, at + i)),
            whole(K * C, C),
            pl.BlockSpec((C, VB), lambda i: (0, i)),
        ],
        out_specs=tuple(whole(n, LO) for n, _ in outs),
        out_shape=tuple(jax.ShapeDtypeStruct((n, LO), dtype) for n, dtype in outs),
        scratch_shapes=[pltpu.VMEM((K * C, VB), BF), pltpu.VMEM((rows, LO), F32)],
        compiler_params=pltpu.CompilerParams(vmem_limit_bytes=24 << 20),
        cost_estimate=pl.CostEstimate(
            flops=2 * K * VB * steps * rows * LO, bytes_accessed=2 << 20, transcendentals=0
        ),
        name="scatter",
    )(after, start, kernel_map, weight, grad_pre[part])


def total_of(parts_ref):
    total = parts_ref[0].astype(F32)
    for g in range(1, GROUPS):
        total = total + parts_ref[g].astype(F32)
    return total.astype(BF)


def sum_parts_kernel(after_ref, parts_ref, out_ref):
    total = total_of(parts_ref)
    for g in range(GROUPS):
        out_ref[g] = total


def sum_parts(after, parts):
    return pl.pallas_call(
        sum_parts_kernel,
        in_specs=[pl.BlockSpec(memory_space=pl.ANY), pl.BlockSpec(memory_space=pltpu.VMEM)],
        out_shape=jax.ShapeDtypeStruct(parts.shape, BF),
        compiler_params=pltpu.CompilerParams(vmem_limit_bytes=8 << 20),
        name="sum_parts",
    )(after, parts)


def fold_kernel(grad_ref, from_low_ref, from_high_ref, lists_ref, parts_ref, out_ref, masked_ref):
    share = total_of(parts_ref)
    hots = []
    for j, part_ref in enumerate((from_low_ref, from_high_ref)):
        rows = lists_ref[:, R + j * F : R + (j + 1) * F]
        masked_banks(part_ref[...], rows >> 8, BANKS, masked_ref, j * F)
        hots.append(onehot_rows(rows & (LO - 1), LO))
    folded = lax.dot_general(
        masked_ref[...], jnp.concatenate(hots, axis=1), NT, preferred_element_type=F32
    )
    total = (grad_ref[...] + folded).astype(BF)
    for g in range(GROUPS):
        out_ref[g, :C, :] = total[(g // 2) * C : (g // 2 + 1) * C, (g % 2) * CAP : (g % 2 + 1) * CAP]
        out_ref[g, C:, :] = share


def fold_faces(table_grad, from_low, from_high, lists, parts):
    return pl.pallas_call(
        fold_kernel,
        out_shape=jax.ShapeDtypeStruct((GROUPS, C + LANES, CAP), BF),
        scratch_shapes=[pltpu.VMEM((BANKS * C, 2 * F), BF)],
        compiler_params=pltpu.CompilerParams(vmem_limit_bytes=16 << 20),
        name="fold",
    )(table_grad, from_low, from_high, lists, parts)


def finish_kernel(scale, back_ref, lists_ref, slot_ref, out_ref, wg_ref, flat_ref):
    table = back_ref[:, :C, :].reshape(GROUPS * C, CAP)
    for b in range(R // LO):
        cols = slice(b * LO, (b + 1) * LO)
        product = jnp.dot(table, onehot_rows(slot_ref[:, cols], CAP), preferred_element_type=F32)
        out_ref[:, cols] = select_banks(product, lists_ref[:, cols], GROUPS).astype(BF)
    for t in range(TILES + 1):
        for i in range(C // 16):
            shard, slot = tile_place(i, t)
            tile = back_ref[shard, C + slot * 16 : C + (slot + 1) * 16, :].astype(F32) * scale
            flat_ref[i * 16 : (i + 1) * 16, t * LANES : (t + 1) * LANES] = tile
    for k in range(K):
        wg_ref[k] = flat_ref[:, k * C : (k + 1) * C]


def finish(returned, lists, slot, scale):
    return pl.pallas_call(
        functools.partial(finish_kernel, scale),
        out_shape=(jax.ShapeDtypeStruct((C, R), BF), jax.ShapeDtypeStruct((K, C, C), F32)),
        scratch_shapes=[pltpu.VMEM((C, (TILES + 1) * LANES), F32)],
        compiler_params=pltpu.CompilerParams(vmem_limit_bytes=24 << 20),
        name="finish",
    )(returned, lists, slot)


def body(points, owners, kernel_maps, face_rows, weight, cotangent):
    points, kernel_map, incoming = points[0, 0], kernel_maps.reshape(K, 1, V), cotangent[0, 0]
    lists = jnp.concatenate([owners.reshape(1, R), face_rows.reshape(1, 2 * F)], axis=1)
    side = lax.axis_size("sy")
    up = [(i, i + 1) for i in range(side - 1)]
    down = [(i + 1, i) for i in range(side - 1)]

    outgoing, slot = place_points(points, lists)
    owned = lax.all_to_all(outgoing, "sx", 0, 0, tiled=True)
    lower, upper = take_faces(owned, lists)
    ghost_low = lax.ppermute(upper, "sy", up)
    ghost_high = lax.ppermute(lower, "sy", down)
    weight_rows = jnp.transpose(weight, (1, 0, 2)).reshape(C, K * C)
    output, *grad_pre, weight_part = forward_pass(
        owned, ghost_low, ghost_high, kernel_map, weight_rows, incoming
    )
    weight_columns = jnp.transpose(weight, (0, 2, 1)).reshape(K * C, C)
    scatter = functools.partial(scatter_part, kernel_map=kernel_map, weight=weight_columns, grad_pre=grad_pre)
    across = lambda array, axis: lax.all_to_all(array, axis, 0, 0, tiled=True)
    parts = across(weight_part, "sx")
    (sums,) = scatter(0, grad_pre[0], grad_pre[0])
    row_sums = sum_parts(sums, parts)
    parts = across(row_sums, "sy")
    (sums,) = scatter(1, row_sums, sums)
    table_grad, to_low, to_high = scatter(2, parts, sums)
    from_low = lax.ppermute(to_high, "sy", up)
    from_high = lax.ppermute(to_low, "sy", down)
    owned_grad = fold_faces(table_grad, from_low, from_high, lists, parts)
    returned = across(owned_grad, "sx")
    scale = 1.0 / math.sqrt(GROUPS * side * V)
    point_grad, weight_grad = finish(returned, lists, slot, scale)
    return (output[None, None], point_grad[None, None], weight_grad)


def solution(mesh):
    split = P("sx", "sy", None, None)
    return jax.shard_map(
        body,
        mesh=mesh,
        in_specs=(split, split, split, split, P(), split),
        out_specs=(split, split, P()),
        check_vma=False,
    )
```
